32 devices in a mesh: section: 2 (over y), ep: 16 (over z, x, core).
Axes of the slice: x: 2, y: 2, z: 4, core: 2. Of those that a mesh axis runs over, the one named last changes fastest.
Arguments:
- entering_rising: bfloat16 [8, 128, 3584], P(None, 'ep'), may hold values from -6 to 6
- entering_falling: bfloat16 [8, 128, 3584], P(None, 'ep'), may hold values from -6 to 6
- norm_gain: float32 [2, 3584], P('section'), may hold values from 0.1 to 1.9
- router: bfloat16 [2, 3584, 8], P('section'), may hold values from -0.09375 to 0.09375
- w_gate: bfloat16 [2, 3584, 8192], P('section', None, 'ep'), may hold values from -0.09375 to 0.09375
- w_up: bfloat16 [2, 3584, 8192], P('section', None, 'ep'), may hold values from -0.09375 to 0.09375
- w_down: bfloat16 [2, 8192, 3584], P('section', 'ep'), may hold values from -0.1875 to 0.1875
- routes_rising: int32 [2, 8, 128, 2], P('section', None, 'ep'), may hold values from 0 to 7, all different within a row; in each aligned block of 8 rows (0 to 7, 8 to 15, ..., all dimensions but the last counted through in order) at most 4 rows name the same one
- routes_falling: int32 [2, 8, 128, 2], P('section', None, 'ep'), may hold values from 0 to 7, all different within a row; in each aligned block of 8 rows (0 to 7, 8 to 15, ..., all dimensions but the last counted through in order) at most 4 rows name the same one
Outputs:
- states_rising: bfloat16 [2, 8, 128, 3584], P('section', None, 'ep')
- states_falling: bfloat16 [2, 8, 128, 3584], P('section', None, 'ep')
The draws below stay inside these ranges and needn't reach their ends.
Inputs may be any that keep to these rules, and one draw needn't show every extreme that they name: `routes_rising`: in each aligned block of 8 tokens (one micro-batch on one device of ep, within one layer) no expert is chosen by more than 4 tokens, a bound that some block reaches; the 2 experts of a token differ. `routes_falling`: in each aligned block of 8 tokens (one micro-batch on one device of ep, within one layer) no expert is chosen by more than 4 tokens, a bound that some block reaches; the 2 experts of a token differ.
All inputs are finite; a program needn't handle non-finite values.
Results may differ from the reference program's by a relative error of at most 0.0081.
Values may be sent and summed in bfloat16 or wider, within the bound.
No kernel may reach another device: no remote copies, remote signals or barrier semaphores. Data moves between devices by JAX's collectives and lax.ppermute only.
A program may use at most 64 MiB of HBM per device.

```python
import math
import jax
import jax.numpy as jnp
import numpy as np
from jax import lax

D = 3584
FF = 1024
SPLIT = 2
TOPK = 2
TOK_MB = 8
MICRO = 8
LAYERS = 2
UNITS = 512
EXPERTS = 8
CAP = 4
TOKENS = 128
N_EP = 16


def steps_of(rng, dims, pieces, least, high):
    level = 1.0
    for position, parts in pieces:
        draws = jax.random.uniform(jax.random.fold_in(jax.random.fold_in(rng, 6), position), (parts,), jnp.float32, least / len(pieces), high / len(pieces))
        level = level * jnp.repeat(jnp.exp(draws), dims[position] // parts).reshape((-1,) + (1,) * (len(dims) - 1 - position))
    return level


def routed_block(key, own, number, rows, number_of, top, bound, lean):
    order = jax.random.permutation(key, number_of)
    heavy_load, common = portions_of(number_of, rows * top, bound, lean, True), portions_of(number_of, rows * top, bound, lean, False)
    places = jnp.arange(number_of)

    def named(sizes, turn):
        used = int((sizes > 0).sum())
        fixed = max(1, used // 4)
        passed = fixed + (places - fixed + turn * (used - fixed)) % max(1, number_of - fixed)
        return jnp.zeros((number_of,), jnp.int32).at[order[jnp.where(places < fixed, places, passed)]].set(jnp.asarray(sizes, jnp.int32))

    sizes = jnp.where(number % 4 == 0, named(heavy_load, number // 4), named(common, number - number // 4 - 1))
    mixed = jax.random.permutation(jax.random.fold_in(own, 3), number_of)
    source_of, sink = mixed[0:number_of // 2 * 2:2], mixed[1:number_of // 2 * 2:2]
    margin = jnp.minimum(sizes[source_of] - 1, bound - sizes[sink]) // 2
    margin = jnp.where((source_of == order[0]) | (sink == order[0]) | (sizes[sink] == 0), 0, jnp.maximum(margin, 0))
    passed = jax.random.randint(jax.random.fold_in(own, 4), (number_of // 2,), 0, 1 << 20) % (margin + 1)
    sizes = sizes.at[source_of].add(-passed).at[sink].add(passed)
    labels = jnp.searchsorted(jnp.cumsum(sizes), jnp.arange(rows * top), side="right").astype(jnp.int32)
    listing = labels.reshape(top, rows).T
    listing = listing[jax.random.permutation(jax.random.fold_in(own, 1), rows)]
    turn = jax.random.randint(jax.random.fold_in(own, 2), (rows, 1), 0, top)
    return jnp.take_along_axis(listing, (jnp.arange(top)[None, :] + turn) % top, axis=1)


def portions_of(number_of, total, limit, skew, full):
    weights = [(1 << 20) // math.isqrt(grade ** skew) + 1 for grade in range(1, number_of + 1)]
    largest = limit if full else min(limit, max(-(-total // number_of), total * weights[0] // sum(weights)))
    least = 1 if total - largest >= number_of - 1 else 0
    holding, rest = [largest] + [least] * (number_of - 1), total - largest - least * (number_of - 1)
    while rest > 0:
        free = [i for i in range(1, number_of) if holding[i] < largest] or [i for i in range(1, number_of) if holding[i] < limit]
        pool, remaining = sum([weights[i] for i in free]), rest
        for i in free:
            extra = min(limit - holding[i], max(1, remaining * weights[i] // pool), rest)
            holding[i] = holding[i] + extra
            rest = rest - extra
    return np.array(holding)


def bell_draw(own_key, extent, spread, most, pieces=(), kind=jnp.bfloat16):
    loudness = steps_of(own_key, extent, pieces, -0.22, 0.18) if pieces else 1.0
    values = jax.random.normal(own_key, extent, jnp.float32) * spread * loudness
    return jnp.minimum(jnp.maximum(values, -most), most).astype(kind)


def setup_inputs(seed: int = 0) -> dict:
    keys = jax.random.split(jax.random.key(seed), 10)
    entering_rising = bell_draw(keys[0], (MICRO, TOKENS, D), 1.0, 6.0, ((1, 16),))
    entering_falling = bell_draw(keys[1], (MICRO, TOKENS, D), 1.0, 6.0, ((1, 16),))
    norm_gain = jnp.clip(1.0 + 0.18 * jax.random.normal(keys[2], (LAYERS, D), jnp.float32), 0.1, 1.9)
    router = bell_draw(keys[3], (LAYERS, D, EXPERTS), D ** -0.5, 0.09375, ((0, 2),))
    w_gate = bell_draw(keys[4], (LAYERS, D, EXPERTS * FF), D ** -0.5, 0.09375, ((0, 2), (2, 16)))
    w_up = bell_draw(keys[5], (LAYERS, D, EXPERTS * FF), D ** -0.5, 0.09375, ((0, 2), (2, 16)))
    w_down = bell_draw(keys[6], (LAYERS, EXPERTS * FF, D), FF ** -0.5, 0.1875, ((0, 2), (1, 16)))
    routes_rising_keys = jax.random.split(jax.random.fold_in(keys[7], 1), LAYERS * MICRO * TOKENS // TOK_MB)
    routes_rising_turns = jax.random.permutation(jax.random.fold_in(keys[7], 3), LAYERS * MICRO * TOKENS // TOK_MB)
    routes_rising = jax.vmap(lambda own, number: routed_block(jax.random.fold_in(keys[7], 2), own, number, TOK_MB, EXPERTS, TOPK, CAP, 1))(routes_rising_keys, routes_rising_turns).reshape((LAYERS, MICRO, TOKENS, TOPK))
    routes_falling_keys = jax.random.split(jax.random.fold_in(keys[8], 1), LAYERS * MICRO * TOKENS // TOK_MB)
    routes_falling_turns = jax.random.permutation(jax.random.fold_in(keys[8], 3), LAYERS * MICRO * TOKENS // TOK_MB)
    routes_falling = jax.vmap(lambda own, number: routed_block(jax.random.fold_in(keys[8], 2), own, number, TOK_MB, EXPERTS, TOPK, CAP, 1))(routes_falling_keys, routes_falling_turns).reshape((LAYERS, MICRO, TOKENS, TOPK))
    return {"entering_rising": entering_rising, "entering_falling": entering_falling, "norm_gain": norm_gain, "router": router, "w_gate": w_gate, "w_up": w_up, "w_down": w_down, "routes_rising": routes_rising, "routes_falling": routes_falling}


route_scale = 2.5
epsilon = 1e-06

def moe_layer(current, picks, gain_row, router_layer, gate_layer, up_layer, down_layer):
    flat_rows = current.reshape(MICRO * TOKENS, D)
    widened = flat_rows.astype(jnp.float32)
    normed = (widened * lax.rsqrt(lax.optimization_barrier(jnp.mean(widened * widened, axis=-1, keepdims=True)) + epsilon) * gain_row).astype(jnp.bfloat16)
    scores = jax.nn.sigmoid(jnp.dot(normed, router_layer, preferred_element_type=jnp.float32))
    flat_picks = picks.reshape(MICRO * TOKENS, TOPK)
    chosen = jnp.take_along_axis(scores, flat_picks, axis=1)
    gate_vals = route_scale * chosen / lax.optimization_barrier(jnp.sum(chosen, axis=1, keepdims=True))
    blocks = MICRO * N_EP
    block_picks = flat_picks.reshape(blocks, TOK_MB * TOPK)
    onehot = (block_picks[:, :, None] == jnp.arange(EXPERTS, dtype=jnp.int32)[None, None, :]).astype(jnp.int32)
    before = jnp.cumsum(onehot, axis=1) - onehot
    slot_index = lax.optimization_barrier(jnp.sum(before * onehot, axis=2))
    block_id = jnp.arange(blocks, dtype=jnp.int32)[:, None]
    target = (block_picks * blocks + block_id) * CAP + slot_index
    source = block_id * TOK_MB + jnp.arange(TOK_MB * TOPK, dtype=jnp.int32)[None, :] // TOPK
    lookup = jnp.full((EXPERTS * blocks * CAP,), MICRO * TOKENS, jnp.int32)
    lookup = lookup.at[target.reshape(-1)].set(source.reshape(-1).astype(jnp.int32))
    padded = jnp.concatenate([normed, jnp.zeros((1, D), jnp.bfloat16)], axis=0)
    gathered = padded[lookup].reshape(EXPERTS, blocks * CAP, D)
    gate_each = gate_layer.reshape(D, EXPERTS, FF).transpose(1, 0, 2)
    up_each = up_layer.reshape(D, EXPERTS, FF).transpose(1, 0, 2)
    down_each = down_layer.reshape(EXPERTS, FF, D)

    def one_expert(operands):
        rows_in, gate_w, up_w, down_w = operands
        summed = jnp.zeros((blocks * CAP, D), jnp.float32)
        for piece in range(SPLIT):
            low_unit = piece * UNITS
            gate_act = jnp.dot(rows_in, gate_w[:, low_unit:low_unit + UNITS], preferred_element_type=jnp.float32)
            upward = jnp.dot(rows_in, up_w[:, low_unit:low_unit + UNITS], preferred_element_type=jnp.float32)
            hidden = (jax.nn.silu(gate_act) * upward).astype(jnp.bfloat16)
            partial_out = jnp.dot(hidden, down_w[low_unit:low_unit + UNITS, :], preferred_element_type=jnp.float32).astype(jnp.bfloat16)
            partial_out = lax.optimization_barrier(partial_out)
            summed = summed + partial_out.astype(jnp.float32)
        return summed
    results = lax.map(one_expert, (gathered, gate_each, up_each, down_each))
    results = results.reshape(EXPERTS * blocks * CAP, D)
    picked = results[target.reshape(-1)].reshape(MICRO * TOKENS, TOPK, D)
    mixed_rows = lax.optimization_barrier(jnp.sum(gate_vals[:, :, None] * picked, axis=1))
    updated = (widened + mixed_rows).astype(jnp.bfloat16)
    updated = lax.optimization_barrier(updated)
    return updated.reshape(MICRO, TOKENS, D)

def reference(entering_rising, entering_falling, norm_gain, router, w_gate, w_up, w_down, routes_rising, routes_falling):

    def apply_layer(current, layer_index, routes_all):
        return moe_layer(current, routes_all[layer_index], norm_gain[layer_index], router[layer_index], w_gate[layer_index], w_up[layer_index], w_down[layer_index])
    rising_list = []
    current = entering_rising
    for layer_index in range(LAYERS):
        current = apply_layer(current, layer_index, routes_rising)
        rising_list.append(current)
    falling_list = [None] * LAYERS
    current = entering_falling
    for layer_index in reversed(range(LAYERS)):
        current = apply_layer(current, layer_index, routes_falling)
        falling_list[layer_index] = current
    return (jnp.stack(rising_list), jnp.stack(falling_list))
```

```python
import jax
import jax.numpy as jnp
from jax import lax
from jax.sharding import PartitionSpec as P

route_scale = 2.5
epsilon = 1e-06
CHUNKS = 1


def flipped(value, axis, mask):
    count = lax.axis_size(axis)
    return lax.ppermute(value, axis, [(i, i ^ mask) for i in range(count)])


def shards(
    entering_rising,
    entering_falling,
    norm_gain,
    router,
    w_gate,
    w_up,
    w_down,
    routes_rising,
    routes_falling,
):
    n_section = lax.axis_size("section")
    n_ep = lax.axis_size("ep")
    section_index = lax.axis_index("section")
    ep_index = lax.axis_index("ep")
    micro_count, tok_count, features = entering_rising.shape
    experts = router.shape[2]
    top_count = routes_rising.shape[3]
    sharers = n_ep // experts
    capacity = 2 * max(1, tok_count * top_count // experts)
    half = n_ep // 2
    chips = half // sharers
    my_half = ep_index // half
    my_chip = (ep_index % half) // sharers
    gain_row = norm_gain[0]
    scorer = router[0]
    gate_w = w_gate[0]
    up_w = w_up[0]
    down_w = w_down[0]
    expert_ids = jnp.arange(experts, dtype=jnp.int32)

    group = micro_count // CHUNKS
    tokens = group * tok_count
    room = group * capacity
    slots = jnp.arange(chips * room, dtype=jnp.int32)

    def columns(picks):
        flat = picks.reshape(picks.shape[:-2] + (tok_count * top_count,))
        same = flat[..., :, None] == flat[..., None, :]
        earlier = jnp.tril(jnp.ones((tok_count * top_count,) * 2, bool), -1)
        place = jnp.sum((same & earlier).astype(jnp.int32), axis=-1)
        local = flat - my_half * chips
        inside = (local >= 0) & (local < chips)
        turn = jnp.arange(micro_count, dtype=jnp.int32)[:, None] % group
        column = (local ^ my_chip) * room + turn * capacity + place
        return jnp.where(inside, column, -1).reshape(picks.shape)

    def normalise(current):
        widened = current.astype(jnp.float32)
        normed = (
            widened
            * lax.rsqrt(jnp.mean(widened * widened, axis=-1, keepdims=True) + epsilon)
            * gain_row
        ).astype(jnp.bfloat16)
        return widened, normed

    def pack(normed, column):
        sender = jnp.any(column[:, :, None] == slots, axis=1).astype(jnp.bfloat16)
        rows = lax.dot_general(
            sender, normed, (((0,), (0,)), ((), ())), preferred_element_type=jnp.float32
        )
        return rows.astype(jnp.bfloat16).reshape(chips, room, features)

    def gates(normed, picks, column):
        scores = jax.nn.sigmoid(jnp.dot(normed, scorer, preferred_element_type=jnp.float32))
        onehot = picks[:, :, None] == expert_ids
        chosen = jnp.sum(jnp.where(onehot, scores[:, None, :], 0.0), axis=2)
        gate_vals = route_scale * chosen / jnp.sum(chosen, axis=1, keepdims=True)
        mixing = jnp.sum(
            jnp.where(column[:, :, None] == slots, gate_vals[:, :, None], 0.0), axis=1
        )
        high = lax.reduce_precision(mixing, 8, 7)
        return jnp.concatenate([high, mixing - high], axis=1).astype(jnp.bfloat16)

    def spread(rows):
        return [rows[0]] + [
            flipped(rows[k], "ep", sharers * k) for k in range(1, chips)
        ]

    def experts_of(blocks):
        mine = jnp.concatenate(blocks, axis=0)
        other = flipped(mine, "ep", 1)
        rows = jnp.concatenate([mine, other], axis=0)
        gate_act = jnp.dot(rows, gate_w, preferred_element_type=jnp.float32)
        upward = jnp.dot(rows, up_w, preferred_element_type=jnp.float32)
        hidden = (jax.nn.silu(gate_act) * upward).astype(jnp.bfloat16)
        part = jnp.dot(hidden, down_w, preferred_element_type=jnp.float32).astype(jnp.bfloat16)
        count = mine.shape[0]
        returned = flipped(part[count:], "ep", 1)
        total = (part[:count].astype(jnp.float32) + returned.astype(jnp.float32)).astype(
            jnp.bfloat16
        )
        return total.reshape(chips, room, features)

    def mix(mixing, blocks):
        rows = jnp.concatenate(blocks, axis=0)
        return jnp.dot(
            mixing, jnp.concatenate([rows, rows], axis=0), preferred_element_type=jnp.float32
        )

    def layer(current, picks, column, far_picks, far_column):
        widened, normed = normalise(current)
        far_normed = flipped(normed, "ep", half)
        near_in = spread(pack(normed, column))
        near_out = experts_of(near_in)
        far_in = spread(pack(far_normed, far_column))
        far_out = experts_of(far_in)
        far_part = mix(gates(far_normed, far_picks, far_column), spread(far_out))
        beyond = flipped(far_part.astype(jnp.bfloat16), "ep", half)
        near_part = mix(gates(normed, picks, column), spread(near_out))
        return (widened + (near_part + beyond.astype(jnp.float32))).astype(jnp.bfloat16)

    ticks = jnp.arange(n_section, dtype=jnp.int32)[:, None, None, None]
    picks = jnp.where(section_index == ticks, routes_rising, routes_falling)
    far_picks = flipped(picks, "ep", half)
    column = columns(picks)
    far_column = columns(far_picks)

    shape = (CHUNKS, tokens, features)
    tables = [a.reshape(n_section, CHUNKS, tokens, top_count) for a in (picks, column, far_picks, far_column)]

    def advance(tick, carry, moved):
        current, kept_rising, kept_falling = carry
        rising, falling = section_index == tick, section_index == n_section - 1 - tick
        here = [lax.dynamic_index_in_dim(a, tick, 0, keepdims=False) for a in tables]
        done = [layer(current[c], *[a[c] for a in here]) for c in range(CHUNKS)]
        kept_rising = [jnp.where(rising, d, k) for d, k in zip(done, kept_rising)]
        kept_falling = [jnp.where(falling, d, k) for d, k in zip(done, kept_falling)]
        return [moved(d, rising) for d in done], kept_rising, kept_falling

    def swapped(done, rising):
        return flipped(done, "section", 1)

    entered = jnp.where(section_index == 0, entering_rising, entering_falling).reshape(shape)
    empty = [jnp.zeros((tokens, features), jnp.bfloat16)] * CHUNKS
    carry = ([entered[c] for c in range(CHUNKS)], empty, empty)
    if n_section == 2:
        carry = advance(0, carry, swapped)
        carry = advance(1, carry, lambda done, rising: done)
    else:

        def body(tick, carry):
            def shifted(done, rising):
                up = lax.ppermute(done, "section", [(i, i + 1) for i in range(n_section - 1)])
                down = lax.ppermute(done, "section", [(i + 1, i) for i in range(n_section - 1)])
                return jnp.where(section_index == tick + 1, up, down)

            return advance(tick, carry, shifted)

        carry = lax.fori_loop(0, n_section, body, carry)
    _, kept_rising, kept_falling = carry
    out = (1, micro_count, tok_count, features)
    return (
        jnp.concatenate(kept_rising, axis=0).reshape(out),
        jnp.concatenate(kept_falling, axis=0).reshape(out),
    )


def solution(mesh):
    return jax.shard_map(
        shards,
        mesh=mesh,
        in_specs=(
            P(None, "ep", None),
            P(None, "ep", None),
            P("section", None),
            P("section", None, None),
            P("section", None, "ep"),
            P("section", None, "ep"),
            P("section", "ep", None),
            P("section", None, "ep", None),
            P("section", None, "ep", None),
        ),
        out_specs=(P("section", None, "ep", None), P("section", None, "ep", None)),
        check_vma=False,
    )
```

```python
import functools

import jax
import jax.numpy as jnp
from jax import lax
from jax.experimental import pallas as pl
from jax.experimental.pallas import tpu as pltpu
from jax.sharding import PartitionSpec as P

route_scale = 2.5
epsilon = 1e-06
CHUNKS = 1
F32 = jnp.float32
BF16 = jnp.bfloat16


def flipped(value, axis, mask):
    count = lax.axis_size(axis)
    return lax.ppermute(value, axis, [(i, i ^ mask) for i in range(count)])


def tiles_of(width, wanted=512):
    step = wanted if width % wanted == 0 else width
    return [pl.ds(low, step) for low in range(0, width, step)]


def slot_columns(picks, where, geometry):
    tok_count, capacity, room, chips = geometry
    tokens = picks.shape[0]
    base, chip = where[0], where[1]
    down = lax.broadcasted_iota(jnp.int32, (tokens, tokens), 0)
    across = lax.broadcasted_iota(jnp.int32, (tokens, tokens), 1)
    earlier = (down // tok_count == across // tok_count) & (across < down)
    chosen = [picks[:, k : k + 1].astype(F32) for k in range(picks.shape[1])]
    rows = [as_row(c, down == across) for c in chosen]
    turn = lax.broadcasted_iota(jnp.int32, (tokens, 1), 0) // tok_count
    columns = []
    for k, own in enumerate(chosen):
        before = sum(jnp.where(earlier & (own == row), 1.0, 0.0) for row in rows)
        place = jnp.sum(before, axis=1, keepdims=True).astype(jnp.int32)
        local = picks[:, k : k + 1] - base
        column = (local ^ chip) * room + turn * capacity + place
        columns.append(jnp.where((local >= 0) & (local < chips), column, -1))
    return columns


def as_row(column, diagonal):
    return jnp.sum(jnp.where(diagonal, column, 0.0), axis=0, keepdims=True)


def pack_rows(normed_ref, picks, where, block_refs, geometry):
    tokens, features = normed_ref.shape
    room = geometry[2]
    down = lax.broadcasted_iota(jnp.int32, (tokens, tokens), 0)
    across = lax.broadcasted_iota(jnp.int32, (tokens, tokens), 1)
    slots = lax.broadcasted_iota(jnp.int32, (len(block_refs) * room, tokens), 0).astype(F32)
    sender = jnp.zeros(slots.shape, F32)
    for column in slot_columns(picks, where, geometry):
        sender += jnp.where(slots == as_row(column.astype(F32), down == across), 1.0, 0.0)
    sender = sender.astype(BF16)
    for part in tiles_of(features):
        rows = jnp.dot(sender, normed_ref[:, part], preferred_element_type=F32).astype(BF16)
        for k, block in enumerate(block_refs):
            block[:, part] = rows[k * room : (k + 1) * room]


def start_kernel(geometry, where, current, picks, gain, normed, *blocks):
    wide = current[...].astype(F32)
    scale = lax.rsqrt(jnp.mean(wide * wide, axis=-1, keepdims=True) + epsilon)
    normed[...] = (wide * scale * gain[...]).astype(BF16)
    pack_rows(normed, picks[...], where, blocks, geometry)


def relay_kernel(geometry, where, normed, picks, *blocks):
    pack_rows(normed, picks[...], where, blocks, geometry)


def gate_kernel(geometry, where, near, near_picks, far, far_picks, scorer, mixing):
    room, chips = geometry[2:]
    for place, (normed, picks_ref) in enumerate(((near, near_picks), (far, far_picks))):
        picks = picks_ref[...]
        tokens, top_count = picks.shape
        raw = lax.dot_general(
            normed[...], scorer[...], (((1,), (1,)), ((), ())), preferred_element_type=F32
        )
        scores = jax.nn.sigmoid(raw)
        ids = lax.broadcasted_iota(jnp.int32, scores.shape, 1)
        chosen = [
            jnp.sum(jnp.where(ids == picks[:, k : k + 1], scores, 0.0), axis=1, keepdims=True)
            for k in range(top_count)
        ]
        total = sum(chosen)
        slots = lax.broadcasted_iota(jnp.int32, (tokens, chips * room), 1)
        mixed = jnp.zeros(slots.shape, F32)
        for score, column in zip(chosen, slot_columns(picks, where, geometry)):
            mixed += jnp.where(slots == column, route_scale * score / total, 0.0)
        high = mixed.astype(BF16)
        mixing[place, 0] = high
        mixing[place, 1] = (mixed - high.astype(F32)).astype(BF16)


def mixed_rows(mixing, place, blocks, part):
    rows = jnp.concatenate([block[:, part] for block in blocks], axis=0)
    return jnp.dot(mixing[place, 0], rows, preferred_element_type=F32) + jnp.dot(
        mixing[place, 1], rows, preferred_element_type=F32
    )


def far_mix_kernel(mixing, *refs):
    *blocks, out = refs
    for part in tiles_of(out.shape[1]):
        out[:, part] = mixed_rows(mixing, 1, blocks, part).astype(BF16)


def finish_kernel(mixing, current, beyond, *refs):
    *blocks, out = refs
    for part in tiles_of(out.shape[1]):
        near = mixed_rows(mixing, 0, blocks, part)
        out[:, part] = (
            current[:, part].astype(F32) + (near + beyond[:, part].astype(F32))
        ).astype(BF16)


def expert_kernel(count, *refs):
    blocks, weights = refs[:count], refs[count : count + 6]
    outs = refs[count + 6 : 2 * count + 6]
    gate_buf, up_buf, down_buf, hidden, sems = refs[2 * count + 6 :]
    features, units = gate_buf.shape[1:]
    room = blocks[0].shape[0]
    inner = tiles_of(units, 256)
    copies = []
    for side in range(2):
        gate_w, up_w, _ = weights[3 * side : 3 * side + 3]
        for part in inner:
            copies.append((gate_w.at[:, part], gate_buf.at[side, :, part]))
            copies.append((up_w.at[:, part], up_buf.at[side, :, part]))
    for side in range(2):
        copies.append((weights[3 * side + 2], down_buf.at[side]))
    copies = [pltpu.make_async_copy(a, b, sems.at[n]) for n, (a, b) in enumerate(copies)]
    for copy in copies:
        copy.start()
    pending = iter(copies)
    rows = jnp.concatenate([block[...] for block in blocks], axis=0)
    for side in range(2):
        for part in inner:
            next(pending).wait()
            next(pending).wait()
            gate_act = jnp.dot(rows, gate_buf[side, :, part], preferred_element_type=F32)
            upward = jnp.dot(rows, up_buf[side, :, part], preferred_element_type=F32)
            hidden[side, :, part] = (jax.nn.silu(gate_act) * upward).astype(BF16)
    next(pending).wait()
    next(pending).wait()
    for part in tiles_of(features):
        total = jnp.dot(hidden[0], down_buf[0, :, part], preferred_element_type=F32) + jnp.dot(
            hidden[1], down_buf[1, :, part], preferred_element_type=F32
        )
        total = total.astype(BF16)
        for k, out in enumerate(outs):
            out[:, part] = total[k * room : (k + 1) * room]


VMEM = pl.BlockSpec(memory_space=pltpu.VMEM)
SMEM = pl.BlockSpec(memory_space=pltpu.SMEM)
HBM = pl.BlockSpec(memory_space=pl.ANY)


def shards(
    entering_rising,
    entering_falling,
    norm_gain,
    router,
    w_gate,
    w_up,
    w_down,
    routes_rising,
    routes_falling,
):
    n_section = lax.axis_size("section")
    n_ep = lax.axis_size("ep")
    section_index = lax.axis_index("section")
    ep_index = lax.axis_index("ep")
    micro_count, tok_count, features = entering_rising.shape
    experts = router.shape[2]
    units = w_gate.shape[2]
    top_count = routes_rising.shape[3]
    sharers = n_ep // experts
    capacity = 2 * max(1, tok_count * top_count // experts)
    half = n_ep // 2
    chips = half // sharers
    where = jnp.stack([ep_index // half * chips, ep_index % half // sharers]).astype(jnp.int32)
    scorer = router[0].T
    own = (w_gate[0], w_up[0], w_down[0])
    weights = own + tuple(flipped(w, "ep", 1) for w in own)

    chunks = CHUNKS if micro_count // CHUNKS * capacity % 16 == 0 else 1
    group = micro_count // chunks
    tokens = group * tok_count
    room = group * capacity
    geometry = (tok_count, capacity, room, chips)
    block = jax.ShapeDtypeStruct((room, features), BF16)
    state = jax.ShapeDtypeStruct((tokens, features), BF16)
    params = pltpu.CompilerParams(vmem_limit_bytes=48 << 20)

    def call(kernel, out_shape, in_specs, flops, moved, scratch=()):
        return pl.pallas_call(
            kernel,
            out_shape=out_shape,
            in_specs=in_specs,
            out_specs=jax.tree.map(lambda _: VMEM, out_shape),
            scratch_shapes=scratch,
            compiler_params=params,
            cost_estimate=pl.CostEstimate(flops=flops, bytes_accessed=moved, transcendentals=0),
        )

    row_bytes = 2 * tokens * features
    pack_flops = 2 * chips * room * tokens * features
    start = call(
        functools.partial(start_kernel, geometry),
        [state] + [block] * chips,
        [SMEM, VMEM, VMEM, VMEM],
        pack_flops,
        4 * row_bytes,
    )
    relay = call(
        functools.partial(relay_kernel, geometry), [block] * chips, [SMEM, VMEM, VMEM], pack_flops, 3 * row_bytes
    )
    gates = call(
        functools.partial(gate_kernel, geometry),
        jax.ShapeDtypeStruct((2, 2, tokens, chips * room), BF16),
        [SMEM, VMEM, VMEM, VMEM, VMEM, VMEM],
        4 * tokens * features * 128,
        2 * row_bytes,
    )
    far_mix = call(far_mix_kernel, state, [VMEM] * (1 + chips), 2 * pack_flops, 3 * row_bytes)
    finish = call(finish_kernel, state, [VMEM] * (3 + chips), 2 * pack_flops, 5 * row_bytes)
    expert = call(
        functools.partial(expert_kernel, chips),
        [block] * chips,
        [VMEM] * chips + [HBM] * 6,
        12 * chips * room * features * units,
        12 * features * units,
        [
            pltpu.VMEM((2, features, units), BF16),
            pltpu.VMEM((2, features, units), BF16),
            pltpu.VMEM((2, units, features), BF16),
            pltpu.VMEM((2, chips * room, units), BF16),
            pltpu.SemaphoreType.DMA((4 * len(tiles_of(units, 256)) + 2,)),
        ],
    )

    def spread(blocks):
        return [blocks[0]] + [flipped(blocks[k], "ep", sharers * k) for k in range(1, chips)]

    def layer(current, picks, far_picks):
        normed, *near_rows = start(where, current, picks, norm_gain)
        far_normed = flipped(normed, "ep", half)
        near_out = expert(*spread(near_rows), *weights)
        far_out = expert(*spread(relay(where, far_normed, far_picks)), *weights)
        mixing = gates(where, normed, picks, far_normed, far_picks, scorer)
        beyond = flipped(far_mix(mixing, *spread(far_out)), "ep", half)
        return finish(mixing, current, beyond, *spread(near_out))

    ticks = jnp.arange(n_section, dtype=jnp.int32)[:, None, None, None]
    picks = jnp.where(section_index == ticks, routes_rising, routes_falling)
    tables = [
        a.reshape(n_section, chunks, tokens, top_count) for a in (picks, flipped(picks, "ep", half))
    ]

    def advance(tick, carry, moved):
        current, kept_rising, kept_falling = carry
        rising, falling = section_index == tick, section_index == n_section - 1 - tick
        here = [lax.dynamic_index_in_dim(a, tick, 0, keepdims=False) for a in tables]
        done = [layer(current[c], *[a[c] for a in here]) for c in range(chunks)]
        kept_rising = [jnp.where(rising, d, k) for d, k in zip(done, kept_rising)]
        kept_falling = [jnp.where(falling, d, k) for d, k in zip(done, kept_falling)]
        return [moved(d, tick) for d in done], kept_rising, kept_falling

    def swapped(done, tick):
        return flipped(done, "section", 1)

    def shifted(done, tick):
        up = lax.ppermute(done, "section", [(i, i + 1) for i in range(n_section - 1)])
        down = lax.ppermute(done, "section", [(i + 1, i) for i in range(n_section - 1)])
        return jnp.where(section_index == tick + 1, up, down)

    shape = (chunks, tokens, features)
    entered = jnp.where(section_index == 0, entering_rising, entering_falling).reshape(shape)
    empty = [jnp.zeros((tokens, features), BF16)] * chunks
    carry = ([entered[c] for c in range(chunks)], empty, empty)
    if n_section == 2:
        carry = advance(0, carry, swapped)
        carry = advance(1, carry, lambda done, tick: done)
    else:
        carry = lax.fori_loop(0, n_section, lambda t, c: advance(t, c, shifted), carry)
    _, kept_rising, kept_falling = carry
    out = (1, micro_count, tok_count, features)
    return (
        jnp.concatenate(kept_rising, axis=0).reshape(out),
        jnp.concatenate(kept_falling, axis=0).reshape(out),
    )


def solution(mesh):
    return jax.shard_map(
        shards,
        mesh=mesh,
        in_specs=(
            P(None, "ep", None),
            P(None, "ep", None),
            P("section", None),
            P("section", None, None),
            P("section", None, "ep"),
            P("section", None, "ep"),
            P("section", "ep", None),
            P("section", None, "ep", None),
            P("section", None, "ep", None),
        ),
        out_specs=(P("section", None, "ep", None), P("section", None, "ep", None)),
        check_vma=False,
    )
```

```python
import functools

import jax
import jax.numpy as jnp
from jax import lax
from jax.experimental import pallas as pl
from jax.experimental.pallas import tpu as pltpu
from jax.sharding import PartitionSpec as P

route_scale = 2.5
epsilon = 1e-06
CHUNKS = 1
EXPERT_VMEM = 50
F32 = jnp.float32
BF16 = jnp.bfloat16


def flipped(value, axis, mask):
    count = lax.axis_size(axis)
    return lax.ppermute(value, axis, [(i, i ^ mask) for i in range(count)])


def tiles_of(width, wanted=512):
    step = wanted if width % wanted == 0 else width
    return [pl.ds(low, step) for low in range(0, width, step)]


def slot_columns(picks, where, geometry):
    tok_count, capacity, room, chips = geometry
    tokens = picks.shape[0]
    base = where[0]
    down = lax.broadcasted_iota(jnp.int32, (tokens, tokens), 0)
    across = lax.broadcasted_iota(jnp.int32, (tokens, tokens), 1)
    earlier = (down // tok_count == across // tok_count) & (across < down)
    chosen = [picks[:, k : k + 1].astype(F32) for k in range(picks.shape[1])]
    rows = [as_row(c, down == across) for c in chosen]
    turn = lax.broadcasted_iota(jnp.int32, (tokens, 1), 0) // tok_count
    columns = []
    for k, own in enumerate(chosen):
        before = sum(jnp.where(earlier & (own == row), 1.0, 0.0) for row in rows)
        place = jnp.sum(before, axis=1, keepdims=True).astype(jnp.int32)
        local = picks[:, k : k + 1] - base
        column = local * room + turn * capacity + place
        columns.append(jnp.where((local >= 0) & (local < chips), column, -1))
    return columns


def as_row(column, diagonal):
    return jnp.sum(jnp.where(diagonal, column, 0.0), axis=0, keepdims=True)


def pack_rows(normed_ref, picks, where, packed, geometry):
    tokens, features = normed_ref.shape
    down = lax.broadcasted_iota(jnp.int32, (tokens, tokens), 0)
    across = lax.broadcasted_iota(jnp.int32, (tokens, tokens), 1)
    slots = lax.broadcasted_iota(jnp.int32, (packed.shape[0], tokens), 0).astype(F32)
    sender = jnp.zeros(slots.shape, F32)
    for column in slot_columns(picks, where, geometry):
        sender += jnp.where(slots == as_row(column.astype(F32), down == across), 1.0, 0.0)
    sender = sender.astype(BF16)
    for part in tiles_of(features):
        packed[:, part] = jnp.dot(
            sender, normed_ref[:, part], preferred_element_type=F32
        ).astype(BF16)


def start_kernel(geometry, where, current, picks, gain, normed, packed):
    wide = current[...].astype(F32)
    scale = lax.rsqrt(jnp.mean(wide * wide, axis=-1, keepdims=True) + epsilon)
    normed[...] = (wide * scale * gain[...]).astype(BF16)
    pack_rows(normed, picks[...], where, packed, geometry)


def relay_kernel(geometry, where, normed, picks, packed):
    pack_rows(normed, picks[...], where, packed, geometry)


def gate_kernel(geometry, where, near, near_picks, far, far_picks, scorer, mixing):
    room, chips = geometry[2:]
    for place, (normed, picks_ref) in enumerate(((near, near_picks), (far, far_picks))):
        picks = picks_ref[...]
        tokens, top_count = picks.shape
        raw = lax.dot_general(
            normed[...], scorer[...], (((1,), (1,)), ((), ())), preferred_element_type=F32
        )
        scores = jax.nn.sigmoid(raw)
        ids = lax.broadcasted_iota(jnp.int32, scores.shape, 1)
        chosen = [
            jnp.sum(jnp.where(ids == picks[:, k : k + 1], scores, 0.0), axis=1, keepdims=True)
            for k in range(top_count)
        ]
        total = sum(chosen)
        slots = lax.broadcasted_iota(jnp.int32, (tokens, chips * room), 1)
        mixed = jnp.zeros(slots.shape, F32)
        for score, column in zip(chosen, slot_columns(picks, where, geometry)):
            mixed += jnp.where(slots == column, route_scale * score / total, 0.0)
        high = mixed.astype(BF16)
        mixing[place, 0] = high
        mixing[place, 1] = (mixed - high.astype(F32)).astype(BF16)


def mixed_rows(mixing, place, returned, part):
    rows = returned[:, part]
    return jnp.dot(mixing[place, 0], rows, preferred_element_type=F32) + jnp.dot(
        mixing[place, 1], rows, preferred_element_type=F32
    )


def far_mix_kernel(mixing, returned, out):
    for part in tiles_of(out.shape[1]):
        out[:, part] = mixed_rows(mixing, 1, returned, part).astype(BF16)


def finish_kernel(mixing, current, beyond, returned, out):
    for part in tiles_of(out.shape[1]):
        near = mixed_rows(mixing, 0, returned, part)
        out[:, part] = (
            current[:, part].astype(F32) + (near + beyond[:, part].astype(F32))
        ).astype(BF16)


def expert_kernel(arrived, *refs):
    weights, (out, gate_buf, up_buf, down_buf, hidden, sems) = refs[:6], refs[6:]
    features, units = gate_buf.shape[1:]
    inner = tiles_of(units, 256)
    copies = []
    for side in range(2):
        gate_w, up_w, _ = weights[3 * side : 3 * side + 3]
        for part in inner:
            copies.append((gate_w.at[:, part], gate_buf.at[side, :, part]))
            copies.append((up_w.at[:, part], up_buf.at[side, :, part]))
    for side in range(2):
        copies.append((weights[3 * side + 2], down_buf.at[side]))
    copies = [pltpu.make_async_copy(a, b, sems.at[n]) for n, (a, b) in enumerate(copies)]
    for copy in copies:
        copy.start()
    pending = iter(copies)
    rows = arrived[...]
    for side in range(2):
        for part in inner:
            next(pending).wait()
            next(pending).wait()
            gate_act = jnp.dot(rows, gate_buf[side, :, part], preferred_element_type=F32)
            upward = jnp.dot(rows, up_buf[side, :, part], preferred_element_type=F32)
            hidden[side, :, part] = (jax.nn.silu(gate_act) * upward).astype(BF16)
    next(pending).wait()
    next(pending).wait()
    for part in tiles_of(features):
        total = jnp.dot(hidden[0], down_buf[0, :, part], preferred_element_type=F32) + jnp.dot(
            hidden[1], down_buf[1, :, part], preferred_element_type=F32
        )
        out[:, part] = total.astype(BF16)


VMEM = pl.BlockSpec(memory_space=pltpu.VMEM)
SMEM = pl.BlockSpec(memory_space=pltpu.SMEM)
HBM = pl.BlockSpec(memory_space=pl.ANY)


def shards(
    entering_rising,
    entering_falling,
    norm_gain,
    router,
    w_gate,
    w_up,
    w_down,
    routes_rising,
    routes_falling,
):
    n_section = lax.axis_size("section")
    n_ep = lax.axis_size("ep")
    section_index = lax.axis_index("section")
    ep_index = lax.axis_index("ep")
    micro_count, tok_count, features = entering_rising.shape
    experts = router.shape[2]
    units = w_gate.shape[2]
    top_count = routes_rising.shape[3]
    sharers = n_ep // experts
    capacity = 2 * max(1, tok_count * top_count // experts)
    half = n_ep // 2
    chips = half // sharers
    where = (ep_index // half * chips).astype(jnp.int32)[None]
    scorer = router[0].T
    own = (w_gate[0], w_up[0], w_down[0])
    weights = own + tuple(flipped(w, "ep", 1) for w in own)

    chunks = CHUNKS if micro_count // CHUNKS * capacity % 16 == 0 else 1
    group = micro_count // chunks
    tokens = group * tok_count
    room = group * capacity
    geometry = (tok_count, capacity, room, chips)
    packed = jax.ShapeDtypeStruct((chips * room, features), BF16)
    state = jax.ShapeDtypeStruct((tokens, features), BF16)

    def call(kernel, out_shape, in_specs, flops, moved, scratch=(), vmem=24):
        return pl.pallas_call(
            kernel,
            out_shape=out_shape,
            in_specs=in_specs,
            out_specs=jax.tree.map(lambda _: VMEM, out_shape),
            scratch_shapes=scratch,
            compiler_params=pltpu.CompilerParams(vmem_limit_bytes=vmem << 20),
            cost_estimate=pl.CostEstimate(flops=flops, bytes_accessed=moved, transcendentals=0),
        )

    row_bytes = 2 * tokens * features
    pack_flops = 2 * chips * room * tokens * features
    start = call(
        functools.partial(start_kernel, geometry),
        [state, packed],
        [SMEM, VMEM, VMEM, VMEM],
        pack_flops,
        4 * row_bytes,
    )
    relay = call(
        functools.partial(relay_kernel, geometry), packed, [SMEM, VMEM, VMEM], pack_flops, 3 * row_bytes
    )
    gates = call(
        functools.partial(gate_kernel, geometry),
        jax.ShapeDtypeStruct((2, 2, tokens, chips * room), BF16),
        [SMEM, VMEM, VMEM, VMEM, VMEM, VMEM],
        4 * tokens * features * 128,
        2 * row_bytes,
    )
    far_mix = call(far_mix_kernel, state, [VMEM, VMEM], 2 * pack_flops, 3 * row_bytes)
    finish = call(finish_kernel, state, [VMEM] * 4, 2 * pack_flops, 5 * row_bytes)
    expert = call(
        expert_kernel,
        packed,
        [VMEM] + [HBM] * 6,
        12 * chips * room * features * units,
        12 * features * units,
        [
            pltpu.VMEM((2, features, units), BF16),
            pltpu.VMEM((2, features, units), BF16),
            pltpu.VMEM((2, units, features), BF16),
            pltpu.VMEM((2, chips * room, units), BF16),
            pltpu.SemaphoreType.DMA((4 * len(tiles_of(units, 256)) + 2,)),
        ],
        EXPERT_VMEM,
    )

    circles = [
        [low + core + sharers * k for k in range(chips)] for low in (0, half) for core in range(sharers)
    ]

    def spread(rows):
        return lax.all_to_all(
            rows, "ep", split_axis=0, concat_axis=0, tiled=True, axis_index_groups=circles
        )

    def layer(current, picks, far_picks):
        normed, near_rows = start(where, current, picks, norm_gain)
        far_normed = flipped(normed, "ep", half)
        near_out = expert(spread(near_rows), *weights)
        far_normed, near_out = lax.optimization_barrier((far_normed, near_out))
        far_out = expert(spread(relay(where, far_normed, far_picks)), *weights)
        mixing = gates(where, normed, picks, far_normed, far_picks, scorer)
        beyond = flipped(far_mix(mixing, spread(far_out)), "ep", half)
        return finish(mixing, current, beyond, spread(near_out))

    ticks = jnp.arange(n_section, dtype=jnp.int32)[:, None, None, None]
    picks = jnp.where(section_index == ticks, routes_rising, routes_falling)
    tables = [
        a.reshape(n_section, chunks, tokens, top_count) for a in (picks, flipped(picks, "ep", half))
    ]

    def advance(tick, carry, moved):
        current, kept_rising, kept_falling = carry
        rising, falling = section_index == tick, section_index == n_section - 1 - tick
        here = [lax.dynamic_index_in_dim(a, tick, 0, keepdims=False) for a in tables]
        done = [layer(current[c], *[a[c] for a in here]) for c in range(chunks)]
        kept_rising = [jnp.where(rising, d, k) for d, k in zip(done, kept_rising)]
        kept_falling = [jnp.where(falling, d, k) for d, k in zip(done, kept_falling)]
        return [moved(d, tick) for d in done], kept_rising, kept_falling

    def swapped(done, tick):
        return flipped(done, "section", 1)

    def shifted(done, tick):
        up = lax.ppermute(done, "section", [(i, i + 1) for i in range(n_section - 1)])
        down = lax.ppermute(done, "section", [(i + 1, i) for i in range(n_section - 1)])
        return jnp.where(section_index == tick + 1, up, down)

    shape = (chunks, tokens, features)
    entered = jnp.where(section_index == 0, entering_rising, entering_falling).reshape(shape)
    empty = [jnp.zeros((tokens, features), BF16)] * chunks
    carry = ([entered[c] for c in range(chunks)], empty, empty)
    if n_section == 2:
        carry = advance(0, carry, swapped)
        carry = advance(1, carry, lambda done, tick: done)
    else:
        carry = lax.fori_loop(0, n_section, lambda t, c: advance(t, c, shifted), carry)
    _, kept_rising, kept_falling = carry
    out = (1, micro_count, tok_count, features)
    return (
        jnp.concatenate(kept_rising, axis=0).reshape(out),
        jnp.concatenate(kept_falling, axis=0).reshape(out),
    )


def solution(mesh):
    return jax.shard_map(
        shards,
        mesh=mesh,
        in_specs=(
            P(None, "ep", None),
            P(None, "ep", None),
            P("section", None),
            P("section", None, None),
            P("section", None, "ep"),
            P("section", None, "ep"),
            P("section", "ep", None),
            P("section", None, "ep", None),
            P("section", None, "ep", None),
        ),
        out_specs=(P("section", None, "ep", None), P("section", None, "ep", None)),
        check_vma=False,
    )
```

```python
import functools

import jax
import jax.numpy as jnp
from jax import lax
from jax.experimental import pallas as pl
from jax.experimental.pallas import tpu as pltpu
from jax.sharding import PartitionSpec as P

route_scale = 2.5
epsilon = 1e-06
CHUNKS = 1
EXPERT_VMEM = 50
F32 = jnp.float32
BF16 = jnp.bfloat16


def flipped(value, axis, mask):
    count = lax.axis_size(axis)
    return lax.ppermute(value, axis, [(i, i ^ mask) for i in range(count)])


def tied(*values):
    return lax.optimization_barrier(values)


def tiles_of(width, wanted=512):
    step = wanted if width % wanted == 0 else width
    return [pl.ds(low, step) for low in range(0, width, step)]


def slot_columns(picks, where, near, geometry):
    tok_count, capacity, room, chips = geometry
    tokens = picks.shape[0]
    base, chip = where[0], where[1] if near else 0
    down = lax.broadcasted_iota(jnp.int32, (tokens, tokens), 0)
    across = lax.broadcasted_iota(jnp.int32, (tokens, tokens), 1)
    earlier = (down // tok_count == across // tok_count) & (across < down)
    chosen = [picks[:, k : k + 1].astype(F32) for k in range(picks.shape[1])]
    rows = [as_row(c, down == across) for c in chosen]
    turn = lax.broadcasted_iota(jnp.int32, (tokens, 1), 0) // tok_count
    columns = []
    for k, own in enumerate(chosen):
        before = sum(jnp.where(earlier & (own == row), 1.0, 0.0) for row in rows)
        place = jnp.sum(before, axis=1, keepdims=True).astype(jnp.int32)
        local = picks[:, k : k + 1] - base
        column = (local ^ chip) * room + turn * capacity + place
        columns.append(jnp.where((local >= 0) & (local < chips), column, -1))
    return columns


def as_row(column, diagonal):
    return jnp.sum(jnp.where(diagonal, column, 0.0), axis=0, keepdims=True)


def start_kernel(near, geometry, where, current, picks, gain, normed, *packed):
    tokens, features = normed.shape
    wide = current[...].astype(F32)
    scale = lax.rsqrt(jnp.mean(wide * wide, axis=-1, keepdims=True) + epsilon)
    normed[...] = (wide * scale * gain[...]).astype(BF16)
    room, chips = geometry[2:]
    down = lax.broadcasted_iota(jnp.int32, (tokens, tokens), 0)
    across = lax.broadcasted_iota(jnp.int32, (tokens, tokens), 1)
    slots = lax.broadcasted_iota(jnp.int32, (chips * room, tokens), 0).astype(F32)
    sender = jnp.zeros(slots.shape, F32)
    for column in slot_columns(picks[...], where, near, geometry):
        sender += jnp.where(slots == as_row(column.astype(F32), down == across), 1.0, 0.0)
    sender = sender.astype(BF16)
    for part in tiles_of(features):
        rows = jnp.dot(sender, normed[:, part], preferred_element_type=F32)
        put_blocks(packed, part, rows.astype(BF16))


def put_blocks(blocks, part, rows):
    room = rows.shape[0] // len(blocks)
    for k, block in enumerate(blocks):
        block[:, part] = rows[k * room : (k + 1) * room]


def get_blocks(blocks, part):
    return jnp.concatenate([block[:, part] for block in blocks], axis=0)


def gate_kernel(geometry, where, near, near_picks, far, far_picks, scorer, mixing):
    room, chips = geometry[2:]
    for place, (normed, picks_ref) in enumerate(((near, near_picks), (far, far_picks))):
        picks = picks_ref[...]
        tokens, top_count = picks.shape
        raw = lax.dot_general(
            normed[...], scorer[...], (((1,), (1,)), ((), ())), preferred_element_type=F32
        )
        scores = jax.nn.sigmoid(raw)
        ids = lax.broadcasted_iota(jnp.int32, scores.shape, 1)
        chosen = [
            jnp.sum(jnp.where(ids == picks[:, k : k + 1], scores, 0.0), axis=1, keepdims=True)
            for k in range(top_count)
        ]
        total = sum(chosen)
        slots = lax.broadcasted_iota(jnp.int32, (tokens, chips * room), 1)
        mixed = jnp.zeros(slots.shape, F32)
        for score, column in zip(chosen, slot_columns(picks, where, place == 0, geometry)):
            mixed += jnp.where(slots == column, route_scale * score / total, 0.0)
        high = mixed.astype(BF16)
        mixing[place, 0] = high
        mixing[place, 1] = (mixed - high.astype(F32)).astype(BF16)


def mixed_rows(mixing, place, returned, part):
    rows = get_blocks(returned, part)
    return jnp.dot(mixing[place, 0], rows, preferred_element_type=F32) + jnp.dot(
        mixing[place, 1], rows, preferred_element_type=F32
    )


def far_mix_kernel(mixing, returned, out):
    for part in tiles_of(out.shape[1]):
        out[:, part] = mixed_rows(mixing, 1, [returned], part).astype(BF16)


def finish_kernel(mixing, current, beyond, *refs):
    *returned, out = refs
    for part in tiles_of(out.shape[1]):
        near = mixed_rows(mixing, 0, returned, part)
        out[:, part] = (
            current[:, part].astype(F32) + (near + beyond[:, part].astype(F32))
        ).astype(BF16)


def expert_kernel(count, *refs):
    arrived, weights, outs = refs[:count], refs[count : count + 6], refs[count + 6 : 2 * count + 6]
    gate_buf, up_buf, down_buf, hidden, sems = refs[2 * count + 6 :]
    features, units = gate_buf.shape[1:]
    inner = tiles_of(units, 256)
    copies = []
    for side in range(2):
        gate_w, up_w, _ = weights[3 * side : 3 * side + 3]
        for part in inner:
            copies.append((gate_w.at[:, part], gate_buf.at[side, :, part]))
            copies.append((up_w.at[:, part], up_buf.at[side, :, part]))
    for part in tiles_of(features):
        for side in range(2):
            copies.append((weights[3 * side + 2].at[:, part], down_buf.at[side, :, part]))
    copies = [pltpu.make_async_copy(a, b, sems.at[n]) for n, (a, b) in enumerate(copies)]
    for copy in copies:
        copy.start()
    pending = iter(copies)
    rows = get_blocks(arrived, slice(None))
    for side in range(2):
        for part in inner:
            next(pending).wait()
            next(pending).wait()
            gate_act = jnp.dot(rows, gate_buf[side, :, part], preferred_element_type=F32)
            upward = jnp.dot(rows, up_buf[side, :, part], preferred_element_type=F32)
            hidden[side, :, part] = (jax.nn.silu(gate_act) * upward).astype(BF16)
    for part in tiles_of(features):
        next(pending).wait()
        next(pending).wait()
        total = jnp.dot(hidden[0], down_buf[0, :, part], preferred_element_type=F32) + jnp.dot(
            hidden[1], down_buf[1, :, part], preferred_element_type=F32
        )
        put_blocks(outs, part, total.astype(BF16))


VMEM = pl.BlockSpec(memory_space=pltpu.VMEM)
SMEM = pl.BlockSpec(memory_space=pltpu.SMEM)
HBM = pl.BlockSpec(memory_space=pl.ANY)


def shards(
    entering_rising,
    entering_falling,
    norm_gain,
    router,
    w_gate,
    w_up,
    w_down,
    routes_rising,
    routes_falling,
):
    n_section = lax.axis_size("section")
    n_ep = lax.axis_size("ep")
    section_index = lax.axis_index("section")
    ep_index = lax.axis_index("ep")
    micro_count, tok_count, features = entering_rising.shape
    experts = router.shape[2]
    units = w_gate.shape[2]
    top_count = routes_rising.shape[3]
    sharers = n_ep // experts
    capacity = 2 * max(1, tok_count * top_count // experts)
    half = n_ep // 2
    chips = half // sharers
    where = jnp.stack([ep_index // half * chips, ep_index % half // sharers]).astype(jnp.int32)
    scorer = router[0].T
    ticks = jnp.arange(n_section, dtype=jnp.int32)[:, None, None, None]
    picks = jnp.where(section_index == ticks, routes_rising, routes_falling)
    own = (w_gate[0], w_up[0], w_down[0])
    picks, far_picks, *own = tied(picks, flipped(picks, "ep", half), *own)
    weights = (*own, *[flipped(w, "ep", 1) for w in own])

    chunks = CHUNKS if micro_count // CHUNKS * capacity % 16 == 0 else 1
    group = micro_count // chunks
    tokens = group * tok_count
    room = group * capacity
    geometry = (tok_count, capacity, room, chips)
    block = jax.ShapeDtypeStruct((room, features), BF16)
    packed = jax.ShapeDtypeStruct((chips * room, features), BF16)
    state = jax.ShapeDtypeStruct((tokens, features), BF16)

    def call(kernel, out_shape, in_specs, flops, moved, scratch=(), vmem=24):
        return pl.pallas_call(
            kernel,
            out_shape=out_shape,
            in_specs=in_specs,
            out_specs=jax.tree.map(lambda _: VMEM, out_shape),
            scratch_shapes=scratch,
            compiler_params=pltpu.CompilerParams(vmem_limit_bytes=vmem << 20),
            cost_estimate=pl.CostEstimate(flops=flops, bytes_accessed=moved, transcendentals=0),
        )

    row_bytes = 2 * tokens * features
    pack_flops = 2 * chips * room * tokens * features
    start, far_start = [
        call(
            functools.partial(start_kernel, near, geometry),
            [state] + shapes,
            [SMEM, VMEM, VMEM, VMEM],
            pack_flops,
            4 * row_bytes,
        )
        for near, shapes in ((True, [block] * chips), (False, [packed]))
    ]
    gates = call(
        functools.partial(gate_kernel, geometry),
        jax.ShapeDtypeStruct((2, 2, tokens, chips * room), BF16),
        [SMEM, VMEM, VMEM, VMEM, VMEM, VMEM],
        4 * tokens * features * 128,
        2 * row_bytes,
    )
    far_mix = call(far_mix_kernel, state, [VMEM, VMEM], 2 * pack_flops, 3 * row_bytes)
    finish = call(finish_kernel, state, [VMEM] * (3 + chips), 2 * pack_flops, 5 * row_bytes)
    expert, far_expert = [
        call(
            functools.partial(expert_kernel, len(shapes)),
            shapes,
            [VMEM] * len(shapes) + [HBM] * 6,
            12 * chips * room * features * units,
            12 * features * units,
            [
                pltpu.VMEM((2, features, units), BF16),
                pltpu.VMEM((2, features, units), BF16),
                pltpu.VMEM((2, units, features), BF16),
                pltpu.VMEM((2, chips * room, units), BF16),
                pltpu.SemaphoreType.DMA(
                    (4 * len(tiles_of(units, 256)) + 2 * len(tiles_of(features)),)
                ),
            ],
            EXPERT_VMEM,
        )
        for shapes in ([block] * chips, [packed])
    ]

    circles = [
        [low + core + sharers * k for k in range(chips)] for low in (0, half) for core in range(sharers)
    ]

    def spread(rows):
        return lax.all_to_all(
            rows, "ep", split_axis=0, concat_axis=0, tiled=True, axis_index_groups=circles
        )

    def pass_on(blocks):
        return [blocks[0]] + [flipped(blocks[k], "ep", sharers * k) for k in range(1, chips)]

    def layer(current, far_current, picks, far_picks):
        normed, *near_rows = start(where, current, picks, norm_gain)
        far_current, *near_rows = tied(far_current, *near_rows)
        far_normed, far_rows = far_start(where, far_current, far_picks, norm_gain)
        mixing = gates(where, normed, picks, far_normed, far_picks, scorer)
        far_in, mixing = tied(spread(far_rows), mixing)
        (far_out,) = far_expert(far_in, *weights)
        far_out, *near_in = tied(far_out, *pass_on(near_rows))
        near_out = expert(*near_in, *weights)
        far_part, *near_out = tied(far_mix(mixing, spread(far_out)), *near_out)
        beyond = flipped(far_part, "ep", half)
        return finish(mixing, current, beyond, *pass_on(near_out))

    tables = [a.reshape(n_section, chunks, tokens, top_count) for a in (picks, far_picks)]

    def swapped(done, tick):
        across = [(i, (i + n_ep) % (2 * n_ep) ^ half) for i in range(2 * n_ep)]
        return flipped(done, "section", 1), lax.ppermute(done, ("section", "ep"), across)

    def advance(tick, carry, moved):
        current, far_current, kept_rising, kept_falling = carry
        rising, falling = section_index == tick, section_index == n_section - 1 - tick
        here = [lax.dynamic_index_in_dim(a, tick, 0, keepdims=False) for a in tables]
        done = [layer(current[c], far_current[c], *[a[c] for a in here]) for c in range(chunks)]
        kept_rising = [jnp.where(rising, d, k) for d, k in zip(done, kept_rising)]
        kept_falling = [jnp.where(falling, d, k) for d, k in zip(done, kept_falling)]
        moves = [moved(d, tick) for d in done]
        return [m[0] for m in moves], [m[1] for m in moves], kept_rising, kept_falling

    def shifted(done, tick):
        up = lax.ppermute(done, "section", [(i, i + 1) for i in range(n_section - 1)])
        down = lax.ppermute(done, "section", [(i + 1, i) for i in range(n_section - 1)])
        here = jnp.where(section_index == tick + 1, up, down)
        return here, flipped(here, "ep", half)

    shape = (chunks, tokens, features)
    entered = jnp.where(section_index == 0, entering_rising, entering_falling).reshape(shape)
    empty = [jnp.zeros((tokens, features), BF16)] * chunks
    entered = [entered[c] for c in range(chunks)]
    carry = (entered, [flipped(e, "ep", half) for e in entered], empty, empty)
    if n_section == 2:
        carry = advance(0, carry, swapped)
        carry = advance(1, carry, lambda done, tick: (done, done))
    else:
        carry = lax.fori_loop(0, n_section, lambda t, c: advance(t, c, shifted), carry)
    _, _, kept_rising, kept_falling = carry
    out = (1, micro_count, tok_count, features)
    return (
        jnp.concatenate(kept_rising, axis=0).reshape(out),
        jnp.concatenate(kept_falling, axis=0).reshape(out),
    )


def solution(mesh):
    return jax.shard_map(
        shards,
        mesh=mesh,
        in_specs=(
            P(None, "ep", None),
            P(None, "ep", None),
            P("section", None),
            P("section", None, None),
            P("section", None, "ep"),
            P("section", None, "ep"),
            P("section", "ep", None),
            P("section", None, "ep", None),
            P("section", None, "ep", None),
        ),
        out_specs=(P("section", None, "ep", None), P("section", None, "ep", None)),
        check_vma=False,
    )
```

```python
import functools

import jax
import jax.numpy as jnp
from jax import lax
from jax.experimental import pallas as pl
from jax.experimental.pallas import tpu as pltpu
from jax.sharding import PartitionSpec as P

route_scale = 2.5
epsilon = 1e-06
EXPERT_VMEM = 50
F32 = jnp.float32
BF16 = jnp.bfloat16


def flipped(value, axis, mask):
    count = lax.axis_size(axis)
    return lax.ppermute(value, axis, [(i, i ^ mask) for i in range(count)])


def tied(*values):
    return lax.optimization_barrier(values)


def after(first, *values):
    return lax.optimization_barrier((first, *values))[1:]


def tiles_of(width, wanted=512):
    step = wanted if width % wanted == 0 else width
    return [pl.ds(low, step) for low in range(0, width, step)]


def slot_columns(picks, where, near, geometry):
    tok_count, capacity, room, chips = geometry
    tokens = picks.shape[0]
    base, chip = where[0], where[1] if near else 0
    down = lax.broadcasted_iota(jnp.int32, (tokens, tokens), 0)
    across = lax.broadcasted_iota(jnp.int32, (tokens, tokens), 1)
    earlier = (down // tok_count == across // tok_count) & (across < down)
    chosen = [picks[:, k : k + 1].astype(F32) for k in range(picks.shape[1])]
    rows = [as_row(c, down == across) for c in chosen]
    turn = lax.broadcasted_iota(jnp.int32, (tokens, 1), 0) // tok_count
    columns = []
    for k, own in enumerate(chosen):
        before = sum(jnp.where(earlier & (own == row), 1.0, 0.0) for row in rows)
        place = jnp.sum(before, axis=1, keepdims=True).astype(jnp.int32)
        local = picks[:, k : k + 1] - base
        column = (local ^ chip) * room + turn * capacity + place
        columns.append(jnp.where((local >= 0) & (local < chips), column, -1))
    return columns


def as_row(column, diagonal):
    return jnp.sum(jnp.where(diagonal, column, 0.0), axis=0, keepdims=True)


def start_kernel(near, geometry, where, current, picks, gain, normed, *packed):
    tokens, features = normed.shape
    wide = current[...].astype(F32)
    scale = lax.rsqrt(jnp.mean(wide * wide, axis=-1, keepdims=True) + epsilon)
    normed[...] = (wide * scale * gain[...]).astype(BF16)
    room, chips = geometry[2:]
    down = lax.broadcasted_iota(jnp.int32, (tokens, tokens), 0)
    across = lax.broadcasted_iota(jnp.int32, (tokens, tokens), 1)
    slots = lax.broadcasted_iota(jnp.int32, (chips * room, tokens), 0).astype(F32)
    sender = jnp.zeros(slots.shape, F32)
    for column in slot_columns(picks[...], where, near, geometry):
        sender += jnp.where(slots == as_row(column.astype(F32), down == across), 1.0, 0.0)
    sender = sender.astype(BF16)
    for part in tiles_of(features):
        rows = jnp.dot(sender, normed[:, part], preferred_element_type=F32)
        put_blocks(packed, part, rows.astype(BF16))


def put_blocks(blocks, part, rows):
    room = rows.shape[0] // len(blocks)
    for k, block in enumerate(blocks):
        block[:, part] = rows[k * room : (k + 1) * room]


def get_blocks(blocks, part):
    return jnp.concatenate([block[:, part] for block in blocks], axis=0)


def gate_kernel(geometry, where, near, near_picks, far_picks, scorer, *refs):
    room, chips = geometry[2:]
    *far, mixing = refs
    for place, (parts, picks_ref) in enumerate((((near,), near_picks), (far, far_picks))):
        picks = picks_ref[...]
        tokens, top_count = picks.shape
        raw = [
            lax.dot_general(
                normed[...], scorer[...], (((1,), (1,)), ((), ())), preferred_element_type=F32
            )
            for normed in parts
        ]
        raw = jnp.concatenate(raw, axis=0)
        scores = jax.nn.sigmoid(raw)
        ids = lax.broadcasted_iota(jnp.int32, scores.shape, 1)
        chosen = [
            jnp.sum(jnp.where(ids == picks[:, k : k + 1], scores, 0.0), axis=1, keepdims=True)
            for k in range(top_count)
        ]
        total = sum(chosen)
        slots = lax.broadcasted_iota(jnp.int32, (tokens, chips * room), 1)
        mixed = jnp.zeros(slots.shape, F32)
        for score, column in zip(chosen, slot_columns(picks, where, place == 0, geometry)):
            mixed += jnp.where(slots == column, route_scale * score / total, 0.0)
        high = mixed.astype(BF16)
        mixing[place, 0] = high
        mixing[place, 1] = (mixed - high.astype(F32)).astype(BF16)


def mixed_rows(mixing, place, returned, part):
    rows = get_blocks(returned, part)
    return jnp.dot(mixing[place, 0], rows, preferred_element_type=F32) + jnp.dot(
        mixing[place, 1], rows, preferred_element_type=F32
    )


def far_mix_kernel(mixing, returned, out):
    for part in tiles_of(out.shape[1]):
        out[:, part] = mixed_rows(mixing, 1, [returned], part).astype(BF16)


def finish_kernel(mixing, current, beyond, *refs):
    *returned, out = refs
    for part in tiles_of(out.shape[1]):
        near = mixed_rows(mixing, 0, returned, part)
        total = current[:, part].astype(F32) + (near + beyond[:, part].astype(F32))
        out[:, part] = total.astype(BF16)


def last_kernel(section, mixing, current, beyond, first, *refs):
    *returned, rising, falling = refs
    for part in tiles_of(first.shape[1]):
        near = mixed_rows(mixing, 0, returned, part)
        last = current[:, part].astype(F32) + (near + beyond[:, part].astype(F32))
        earlier = first[:, part].astype(F32)
        rising[:, part] = jnp.where(section[0] == 0, earlier, last).astype(BF16)
        falling[:, part] = jnp.where(section[0] == 0, last, earlier).astype(BF16)


def expert_kernel(sources, chips, *refs):
    arrived, weights, refs = refs[:sources], refs[sources : sources + 6], refs[sources + 6 :]
    *outs, gate_buf, up_buf, down_buf, hidden, sems = refs
    features, units = gate_buf.shape[1:]
    inner = tiles_of(units, 256)
    copies = []
    for side in range(2):
        gate_w, up_w, _ = weights[3 * side : 3 * side + 3]
        for part in inner:
            copies.append((gate_w.at[:, part], gate_buf.at[side, :, part]))
            copies.append((up_w.at[:, part], up_buf.at[side, :, part]))
    for part in tiles_of(features):
        for side in range(2):
            copies.append((weights[3 * side + 2].at[:, part], down_buf.at[side, :, part]))
    copies = [pltpu.make_async_copy(a, b, sems.at[n]) for n, (a, b) in enumerate(copies)]
    for copy in copies:
        copy.start()
    pending = iter(copies)
    if chips:
        share = arrived[0].shape[0] // chips
        rows = jnp.concatenate(
            [piece[k * share : (k + 1) * share] for k in range(chips) for piece in arrived], axis=0
        )
    else:
        rows = get_blocks(arrived, slice(None))
    for side in range(2):
        for part in inner:
            next(pending).wait()
            next(pending).wait()
            gate_act = jnp.dot(rows, gate_buf[side, :, part], preferred_element_type=F32)
            upward = jnp.dot(rows, up_buf[side, :, part], preferred_element_type=F32)
            hidden[side, :, part] = (jax.nn.silu(gate_act) * upward).astype(BF16)
    for part in tiles_of(features):
        next(pending).wait()
        next(pending).wait()
        total = jnp.dot(hidden[0], down_buf[0, :, part], preferred_element_type=F32) + jnp.dot(
            hidden[1], down_buf[1, :, part], preferred_element_type=F32
        )
        put_blocks(outs, part, total.astype(BF16))


VMEM = pl.BlockSpec(memory_space=pltpu.VMEM)
SMEM = pl.BlockSpec(memory_space=pltpu.SMEM)
HBM = pl.BlockSpec(memory_space=pl.ANY)


def shards(
    entering_rising,
    entering_falling,
    norm_gain,
    router,
    w_gate,
    w_up,
    w_down,
    routes_rising,
    routes_falling,
):
    n_section = lax.axis_size("section")
    n_ep = lax.axis_size("ep")
    section_index = lax.axis_index("section")
    ep_index = lax.axis_index("ep")
    micro_count, tok_count, features = entering_rising.shape
    experts = router.shape[2]
    units = w_gate.shape[2]
    top_count = routes_rising.shape[3]
    sharers = n_ep // experts
    capacity = 2 * max(1, tok_count * top_count // experts)
    half = n_ep // 2
    chips = half // sharers
    where = jnp.stack([ep_index // half * chips, ep_index % half // sharers]).astype(jnp.int32)
    scorer = router[0].T
    ticks = jnp.arange(n_section, dtype=jnp.int32)[:, None, None, None]
    picks = jnp.where(section_index == ticks, routes_rising, routes_falling)
    own = (w_gate[0], w_up[0], w_down[0])
    far_picks = flipped(picks, "ep", half)

    tokens = micro_count * tok_count
    room = micro_count * capacity
    geometry = (tok_count, capacity, room, chips)
    block = jax.ShapeDtypeStruct((room, features), BF16)
    packed = jax.ShapeDtypeStruct((chips * room, features), BF16)
    state = jax.ShapeDtypeStruct((tokens, features), BF16)

    def call(kernel, out_shape, in_specs, flops, moved, scratch=(), vmem=24):
        return pl.pallas_call(
            kernel,
            out_shape=out_shape,
            in_specs=in_specs,
            out_specs=jax.tree.map(lambda _: VMEM, out_shape),
            scratch_shapes=scratch,
            compiler_params=pltpu.CompilerParams(vmem_limit_bytes=vmem << 20),
            cost_estimate=pl.CostEstimate(flops=flops, bytes_accessed=moved, transcendentals=0),
        )

    row_bytes = 2 * tokens * features
    pack_flops = 2 * chips * room * tokens * features
    start = call(
        functools.partial(start_kernel, True, geometry),
        [state] + [block] * chips,
        [SMEM, VMEM, VMEM, VMEM],
        pack_flops,
        4 * row_bytes,
    )

    def far_start(cut):
        piece = jax.ShapeDtypeStruct((tokens // cut, features), BF16)
        some = jax.ShapeDtypeStruct((chips * room // cut, features), BF16)
        return call(
            functools.partial(start_kernel, False, (tok_count, capacity, room // cut, chips)),
            [piece, some],
            [SMEM, VMEM, VMEM, VMEM],
            pack_flops // cut,
            4 * row_bytes // cut,
        )

    def gates(cut):
        return call(
            functools.partial(gate_kernel, geometry),
            jax.ShapeDtypeStruct((2, 2, tokens, chips * room), BF16),
            [SMEM] + [VMEM] * (4 + cut),
            4 * tokens * features * 128,
            2 * row_bytes,
        )

    def expert(sources, joined, shapes):
        return call(
            functools.partial(expert_kernel, sources, joined),
            shapes,
            [VMEM] * sources + [HBM] * 6,
            12 * chips * room * features * units,
            12 * features * units,
            [
                pltpu.VMEM((2, features, units), BF16),
                pltpu.VMEM((2, features, units), BF16),
                pltpu.VMEM((2, units, features), BF16),
                pltpu.VMEM((2, chips * room, units), BF16),
                pltpu.SemaphoreType.DMA(
                    (4 * len(tiles_of(units, 256)) + 2 * len(tiles_of(features)),)
                ),
            ],
            EXPERT_VMEM,
        )

    far_mix = call(far_mix_kernel, state, [VMEM, VMEM], 2 * pack_flops, 3 * row_bytes)
    finish_last = call(
        last_kernel, [state] * 2, [SMEM] + [VMEM] * (4 + chips), 2 * pack_flops, 7 * row_bytes
    )
    finish = call(
        finish_kernel, state, [VMEM] * (3 + chips), 2 * pack_flops, 5 * row_bytes)
    circles = [
        [low + core + sharers * k for k in range(chips)] for low in (0, half) for core in range(sharers)
    ]

    def spread(rows):
        return lax.all_to_all(
            rows, "ep", split_axis=0, concat_axis=0, tiled=True, axis_index_groups=circles
        )

    def pass_on(blocks):
        return [blocks[0]] + [flipped(blocks[k], "ep", sharers * k) for k in range(1, chips)]

    def layer(current, far_current, picks, far_picks, weights):
        normed, *near_rows = start(where, current, picks, norm_gain)
        far_current = list(far_current)
        pieces = len(far_current)
        far_current[-1], *near_rows = tied(far_current[-1], *near_rows)
        far_in, far_normed = [], []
        for states, chosen in zip(far_current, jnp.split(far_picks, pieces)):
            part, rows = far_start(pieces)(where, states, chosen, norm_gain)
            far_normed.append(part)
            far_in.append(spread(rows))
        mixing = gates(pieces)(where, normed, picks, far_picks, scorer, *far_normed)
        far_in[-1], mixing, *near_rows = tied(far_in[-1], mixing, *near_rows)
        (far_out,) = expert(pieces, chips, [packed])(*far_in, *weights)
        far_out, *near_in = tied(far_out, *pass_on(near_rows))
        near_out = expert(chips, 0, [block] * chips)(*near_in, *weights)
        far_part, *near_out = tied(far_mix(mixing, spread(far_out)), *near_out)
        beyond = flipped(far_part, "ep", half)
        return mixing, current, beyond, pass_on(near_out)

    tables = [a.reshape(n_section, tokens, top_count) for a in (picks, far_picks)]

    def advance(tick, current, far_current, weights):
        here = [lax.dynamic_index_in_dim(a, tick, 0, keepdims=False) for a in tables]
        return layer(current, far_current, *here, weights)

    def whole_weights(*own):
        return (*own, *[flipped(w, "ep", 1) for w in own])

    entered = jnp.where(section_index == 0, entering_rising, entering_falling)
    entered = entered.reshape(tokens, features)
    pieces = 2 if room % 32 == 0 and n_section == 2 else 1
    far = [flipped(e, "ep", half) for e in jnp.split(entered, pieces)]
    weights = whole_weights(*own)
    if n_section == 2:
        mixing, current, beyond, returned = advance(0, entered, far, weights)
        first = finish(mixing, current, beyond, *returned)
        across = [(i, (i + n_ep) % (2 * n_ep) ^ half) for i in range(2 * n_ep)]
        far = [lax.ppermute(first, ("section", "ep"), across)]
        mixing, current, beyond, returned = advance(1, flipped(first, "section", 1), far, weights)
        here = section_index.astype(jnp.int32)[None]
        kept_rising, kept_falling = finish_last(here, mixing, current, beyond, first, *returned)
    else:

        def body(tick, carry):
            current, far, kept_rising, kept_falling = carry
            mixing, current, beyond, returned = advance(tick, current, far, weights)
            done = finish(mixing, current, beyond, *returned)
            kept_rising = jnp.where(section_index == tick, done, kept_rising)
            kept_falling = jnp.where(section_index == n_section - 1 - tick, done, kept_falling)
            up = lax.ppermute(done, "section", [(i, i + 1) for i in range(n_section - 1)])
            down = lax.ppermute(done, "section", [(i + 1, i) for i in range(n_section - 1)])
            current = jnp.where(section_index == tick + 1, up, down)
            far = [flipped(current, "ep", half)]
            return current, far, kept_rising, kept_falling

        empty = jnp.zeros((tokens, features), BF16)
        _, _, kept_rising, kept_falling = lax.fori_loop(
            0, n_section, body, (entered, far, empty, empty)
        )
    out = (1, micro_count, tok_count, features)
    return (
        kept_rising.reshape(out),
        kept_falling.reshape(out),
    )


def solution(mesh):
    return jax.shard_map(
        shards,
        mesh=mesh,
        in_specs=(
            P(None, "ep", None),
            P(None, "ep", None),
            P("section", None),
            P("section", None, None),
            P("section", None, "ep"),
            P("section", None, "ep"),
            P("section", "ep", None),
            P("section", None, "ep", None),
            P("section", None, "ep", None),
        ),
        out_specs=(P("section", None, "ep", None), P("section", None, "ep", None)),
        check_vma=False,
    )
```

```python
import functools

import jax
import jax.numpy as jnp
from jax import lax
from jax.experimental import pallas as pl
from jax.experimental.pallas import tpu as pltpu
from jax.sharding import PartitionSpec as P

route_scale = 2.5
epsilon = 1e-06
EXPERT_VMEM = 50
F32 = jnp.float32
BF16 = jnp.bfloat16


def flipped(value, axis, mask):
    count = lax.axis_size(axis)
    return lax.ppermute(value, axis, [(i, i ^ mask) for i in range(count)])


def tied(*values):
    return lax.optimization_barrier(values)


def after(first, *values):
    return lax.optimization_barrier((first, *values))[1:]


def tiles_of(width, wanted=512):
    step = wanted if width % wanted == 0 else width
    return [pl.ds(low, step) for low in range(0, width, step)]


def slot_columns(picks, where, near, geometry):
    tok_count, capacity, room, chips = geometry
    tokens = picks.shape[0]
    base, chip = where[0], where[1] if near else 0
    down = lax.broadcasted_iota(jnp.int32, (tokens, tokens), 0)
    across = lax.broadcasted_iota(jnp.int32, (tokens, tokens), 1)
    earlier = (down // tok_count == across // tok_count) & (across < down)
    chosen = [picks[:, k : k + 1].astype(F32) for k in range(picks.shape[1])]
    rows = [as_row(c, down == across) for c in chosen]
    turn = lax.broadcasted_iota(jnp.int32, (tokens, 1), 0) // tok_count
    columns = []
    for k, own in enumerate(chosen):
        before = sum(jnp.where(earlier & (own == row), 1.0, 0.0) for row in rows)
        place = jnp.sum(before, axis=1, keepdims=True).astype(jnp.int32)
        local = picks[:, k : k + 1] - base
        column = (local ^ chip) * room + turn * capacity + place
        columns.append(jnp.where((local >= 0) & (local < chips), column, -1))
    return columns


def as_row(column, diagonal):
    return jnp.sum(jnp.where(diagonal, column, 0.0), axis=0, keepdims=True)


def start_kernel(near, geometry, where, current, picks, gain, normed, *packed):
    tokens, features = normed.shape
    wide = current[...].astype(F32)
    scale = lax.rsqrt(jnp.mean(wide * wide, axis=-1, keepdims=True) + epsilon)
    normed[...] = (wide * scale * gain[...]).astype(BF16)
    room, chips = geometry[2:]
    down = lax.broadcasted_iota(jnp.int32, (tokens, tokens), 0)
    across = lax.broadcasted_iota(jnp.int32, (tokens, tokens), 1)
    slots = lax.broadcasted_iota(jnp.int32, (chips * room, tokens), 0).astype(F32)
    sender = jnp.zeros(slots.shape, F32)
    for column in slot_columns(picks[...], where, near, geometry):
        sender += jnp.where(slots == as_row(column.astype(F32), down == across), 1.0, 0.0)
    sender = sender.astype(BF16)
    for part in tiles_of(features):
        rows = jnp.dot(sender, normed[:, part], preferred_element_type=F32)
        put_blocks(packed, part, rows.astype(BF16))


def put_blocks(blocks, part, rows):
    room = rows.shape[0] // len(blocks)
    for k, block in enumerate(blocks):
        block[:, part] = rows[k * room : (k + 1) * room]


def get_blocks(blocks, part):
    return jnp.concatenate([block[:, part] for block in blocks], axis=0)


def gate_kernel(turned, geometry, where, near, near_picks, far_picks, scorer, *refs):
    room, chips = geometry[2:]
    *far, mixing = refs
    for place, (parts, picks_ref) in enumerate((((near,), near_picks), (far, far_picks))):
        picks = picks_ref[...]
        tokens, top_count = picks.shape
        raw = [
            lax.dot_general(
                normed[...], scorer[...], (((1,), (1,)), ((), ())), preferred_element_type=F32
            )
            for normed in parts
        ]
        raw = jnp.concatenate(raw, axis=0)
        scores = jax.nn.sigmoid(raw)
        ids = lax.broadcasted_iota(jnp.int32, scores.shape, 1)
        chosen = [
            jnp.sum(jnp.where(ids == picks[:, k : k + 1], scores, 0.0), axis=1, keepdims=True)
            for k in range(top_count)
        ]
        total = sum(chosen)
        slots = lax.broadcasted_iota(jnp.int32, (tokens, chips * room), 1)
        mixed = jnp.zeros(slots.shape, F32)
        for score, column in zip(chosen, slot_columns(picks, where, turned or place == 0, geometry)):
            mixed += jnp.where(slots == column, route_scale * score / total, 0.0)
        high = mixed.astype(BF16)
        mixing[place, 0] = high
        mixing[place, 1] = (mixed - high.astype(F32)).astype(BF16)


def mixed_rows(mixing, place, returned, part):
    rows = get_blocks(returned, part)
    return jnp.dot(mixing[place, 0], rows, preferred_element_type=F32) + jnp.dot(
        mixing[place, 1], rows, preferred_element_type=F32
    )


def far_mix_kernel(mixing, *refs):
    *returned, out = refs
    for part in tiles_of(out.shape[1]):
        out[:, part] = mixed_rows(mixing, 1, returned, part).astype(BF16)


def finish_kernel(mixing, current, beyond, *refs):
    *returned, out = refs
    for part in tiles_of(out.shape[1]):
        near = mixed_rows(mixing, 0, returned, part)
        total = current[:, part].astype(F32) + (near + beyond[:, part].astype(F32))
        out[:, part] = total.astype(BF16)


def last_kernel(section, mixing, current, beyond, first, *refs):
    *returned, rising, falling = refs
    for part in tiles_of(first.shape[1]):
        near = mixed_rows(mixing, 0, returned, part)
        last = current[:, part].astype(F32) + (near + beyond[:, part].astype(F32))
        earlier = first[:, part].astype(F32)
        rising[:, part] = jnp.where(section[0] == 0, earlier, last).astype(BF16)
        falling[:, part] = jnp.where(section[0] == 0, last, earlier).astype(BF16)


def joined_rows(arrived, chips):
    if not chips:
        return get_blocks(arrived, slice(None))
    share = arrived[0].shape[0] // chips
    return jnp.concatenate(
        [piece[k * share : (k + 1) * share] for k in range(chips) for piece in arrived], axis=0
    )


def expert_kernel(sources, chips, *refs):
    arrived, weights, refs = refs[:sources], refs[sources : sources + 6], refs[sources + 6 :]
    *outs, gate_buf, up_buf, down_buf, hidden, sems = refs
    features, units = gate_buf.shape[1:]
    copies = []
    for side in range(2):
        gate_w, up_w, _ = weights[3 * side : 3 * side + 3]
        for part in tiles_of(units, 256):
            copies.append((gate_w.at[:, part], gate_buf.at[side, :, part]))
            copies.append((up_w.at[:, part], up_buf.at[side, :, part]))
    for part in tiles_of(features):
        for side in range(2):
            copies.append((weights[3 * side + 2].at[:, part], down_buf.at[side, :, part]))
    copies = [pltpu.make_async_copy(a, b, sems.at[n]) for n, (a, b) in enumerate(copies)]
    for copy in copies:
        copy.start()
    pending = iter(copies)

    def ready():
        next(pending).wait()
        next(pending).wait()

    held = [buf.at[side] for side in range(2) for buf in (gate_buf, up_buf, down_buf)]
    serve(joined_rows(arrived, chips), held, hidden, outs, ready)


def serve(rows, weights, hidden, outs, ready):
    for side in range(2):
        gate_w, up_w, _ = weights[3 * side : 3 * side + 3]
        for part in tiles_of(hidden.shape[2], 256):
            ready()
            gate_act = jnp.dot(rows, gate_w[:, part], preferred_element_type=F32)
            upward = jnp.dot(rows, up_w[:, part], preferred_element_type=F32)
            hidden[side, :, part] = (jax.nn.silu(gate_act) * upward).astype(BF16)
    for part in tiles_of(outs[0].shape[1]):
        ready()
        total = jnp.dot(hidden[0], weights[2][:, part], preferred_element_type=F32) + jnp.dot(
            hidden[1], weights[5][:, part], preferred_element_type=F32
        )
        put_blocks(outs, part, total.astype(BF16))


VMEM = pl.BlockSpec(memory_space=pltpu.VMEM)
SMEM = pl.BlockSpec(memory_space=pltpu.SMEM)
HBM = pl.BlockSpec(memory_space=pl.ANY)


def shards(
    entering_rising,
    entering_falling,
    norm_gain,
    router,
    w_gate,
    w_up,
    w_down,
    routes_rising,
    routes_falling,
):
    n_section = lax.axis_size("section")
    n_ep = lax.axis_size("ep")
    section_index = lax.axis_index("section")
    ep_index = lax.axis_index("ep")
    micro_count, tok_count, features = entering_rising.shape
    experts = router.shape[2]
    units = w_gate.shape[2]
    top_count = routes_rising.shape[3]
    sharers = n_ep // experts
    capacity = 2 * max(1, tok_count * top_count // experts)
    half = n_ep // 2
    chips = half // sharers
    where = jnp.stack([ep_index // half * chips, ep_index % half // sharers]).astype(jnp.int32)
    scorer = router[0].T
    ticks = jnp.arange(n_section, dtype=jnp.int32)[:, None, None, None]
    picks = jnp.where(section_index == ticks, routes_rising, routes_falling)
    own = (w_gate[0], w_up[0], w_down[0])
    far_picks = flipped(picks, "ep", half)

    tokens = micro_count * tok_count
    room = micro_count * capacity
    geometry = (tok_count, capacity, room, chips)
    block = jax.ShapeDtypeStruct((room, features), BF16)
    packed = jax.ShapeDtypeStruct((chips * room, features), BF16)
    state = jax.ShapeDtypeStruct((tokens, features), BF16)

    def call(kernel, out_shape, in_specs, flops, moved, scratch=(), vmem=24):
        return pl.pallas_call(
            kernel,
            out_shape=out_shape,
            in_specs=in_specs,
            out_specs=jax.tree.map(lambda _: VMEM, out_shape),
            scratch_shapes=scratch,
            compiler_params=pltpu.CompilerParams(vmem_limit_bytes=vmem << 20),
            cost_estimate=pl.CostEstimate(flops=flops, bytes_accessed=moved, transcendentals=0),
        )

    row_bytes = 2 * tokens * features
    pack_flops = 2 * chips * room * tokens * features
    start = call(
        functools.partial(start_kernel, True, geometry),
        [state] + [block] * chips,
        [SMEM, VMEM, VMEM, VMEM],
        pack_flops,
        4 * row_bytes,
    )

    def far_start(cut):
        piece = jax.ShapeDtypeStruct((tokens // cut, features), BF16)
        some = jax.ShapeDtypeStruct((chips * room // cut, features), BF16)
        return call(
            functools.partial(start_kernel, False, (tok_count, capacity, room // cut, chips)),
            [piece, some],
            [SMEM, VMEM, VMEM, VMEM],
            pack_flops // cut,
            4 * row_bytes // cut,
        )

    def gates(cut):
        return call(
            functools.partial(gate_kernel, cut == 1, geometry),
            jax.ShapeDtypeStruct((2, 2, tokens, chips * room), BF16),
            [SMEM] + [VMEM] * (4 + cut),
            4 * tokens * features * 128,
            2 * row_bytes,
        )

    def expert(sources, joined, shapes):
        return call(
            functools.partial(expert_kernel, sources, joined),
            shapes,
            [VMEM] * sources + [HBM] * 6,
            12 * chips * room * features * units,
            12 * features * units,
            [
                pltpu.VMEM((2, features, units), BF16),
                pltpu.VMEM((2, features, units), BF16),
                pltpu.VMEM((2, units, features), BF16),
                pltpu.VMEM((2, chips * room, units), BF16),
                pltpu.SemaphoreType.DMA(
                    (4 * len(tiles_of(units, 256)) + 2 * len(tiles_of(features)),)
                ),
            ],
            EXPERT_VMEM,
        )

    def far_mix(mixing, *returned):
        specs = [VMEM] * (1 + len(returned))
        return call(far_mix_kernel, state, specs, 2 * pack_flops, 3 * row_bytes)(mixing, *returned)

    finish_last = call(
        last_kernel, [state] * 2, [SMEM] + [VMEM] * (4 + chips), 2 * pack_flops, 7 * row_bytes
    )
    finish = call(
        finish_kernel, state, [VMEM] * (3 + chips), 2 * pack_flops, 5 * row_bytes)
    circles = [
        [low + core + sharers * k for k in range(chips)] for low in (0, half) for core in range(sharers)
    ]

    def spread(rows):
        return lax.all_to_all(
            rows, "ep", split_axis=0, concat_axis=0, tiled=True, axis_index_groups=circles
        )

    def pass_on(blocks):
        return [blocks[0]] + [flipped(blocks[k], "ep", sharers * k) for k in range(1, chips)]

    def layer(current, far_current, picks, far_picks, weights):
        normed, *near_rows = start(where, current, picks, norm_gain)
        far_current = list(far_current)
        pieces = len(far_current)
        far_current[-1], *near_rows = tied(far_current[-1], *near_rows)
        if pieces == 1:
            normed_far, *rows = start(where, far_current[0], far_picks, norm_gain)
            mixing = gates(1)(where, normed, picks, far_picks, scorer, normed_far)
            far_in = pass_on(rows)
            far_in[-1], mixing, *near_rows = tied(far_in[-1], mixing, *near_rows)
            far_out = list(expert(chips, 0, [block] * chips)(*far_in, *weights))
            far_out[-1], *near_in = tied(far_out[-1], *pass_on(near_rows))
            near_out = expert(chips, 0, [block] * chips)(*near_in, *weights)
            far_part, *near_out = tied(far_mix(mixing, *pass_on(far_out)), *near_out)
        else:
            far_in, far_normed = [], []
            for states, chosen in zip(far_current, jnp.split(far_picks, pieces)):
                part, rows = far_start(pieces)(where, states, chosen, norm_gain)
                far_normed.append(part)
                far_in.append(spread(rows))
            mixing = gates(pieces)(where, normed, picks, far_picks, scorer, *far_normed)
            far_in[-1], mixing, *near_rows = tied(far_in[-1], mixing, *near_rows)
            (far_out,) = expert(pieces, chips, [packed])(*far_in, *weights)
            far_out, *near_in = tied(far_out, *pass_on(near_rows))
            near_out = expert(chips, 0, [block] * chips)(*near_in, *weights)
            far_part, *near_out = tied(far_mix(mixing, spread(far_out)), *near_out)
        beyond = flipped(far_part, "ep", half)
        return mixing, current, beyond, pass_on(near_out)

    tables = [a.reshape(n_section, tokens, top_count) for a in (picks, far_picks)]

    def advance(tick, current, far_current, weights):
        here = [lax.dynamic_index_in_dim(a, tick, 0, keepdims=False) for a in tables]
        return layer(current, far_current, *here, weights)

    def whole_weights(*own):
        return (*own, *[flipped(w, "ep", 1) for w in own])

    entered = jnp.where(section_index == 0, entering_rising, entering_falling)
    entered = entered.reshape(tokens, features)
    pieces = 2 if room % 32 == 0 and n_section == 2 else 1
    far = [flipped(e, "ep", half) for e in jnp.split(entered, pieces)]
    weights = whole_weights(*own)
    if n_section == 2:
        mixing, current, beyond, returned = advance(0, entered, far, weights)
        first = finish(mixing, current, beyond, *returned)
        across = [(i, (i + n_ep) % (2 * n_ep) ^ half) for i in range(2 * n_ep)]
        far = [lax.ppermute(first, ("section", "ep"), across)]
        mixing, current, beyond, returned = advance(1, flipped(first, "section", 1), far, weights)
        here = section_index.astype(jnp.int32)[None]
        kept_rising, kept_falling = finish_last(here, mixing, current, beyond, first, *returned)
    else:

        def body(tick, carry):
            current, far, kept_rising, kept_falling = carry
            mixing, current, beyond, returned = advance(tick, current, far, weights)
            done = finish(mixing, current, beyond, *returned)
            kept_rising = jnp.where(section_index == tick, done, kept_rising)
            kept_falling = jnp.where(section_index == n_section - 1 - tick, done, kept_falling)
            up = lax.ppermute(done, "section", [(i, i + 1) for i in range(n_section - 1)])
            down = lax.ppermute(done, "section", [(i + 1, i) for i in range(n_section - 1)])
            current = jnp.where(section_index == tick + 1, up, down)
            far = [flipped(current, "ep", half)]
            return current, far, kept_rising, kept_falling

        empty = jnp.zeros((tokens, features), BF16)
        _, _, kept_rising, kept_falling = lax.fori_loop(
            0, n_section, body, (entered, far, empty, empty)
        )
    out = (1, micro_count, tok_count, features)
    return (
        kept_rising.reshape(out),
        kept_falling.reshape(out),
    )


def solution(mesh):
    return jax.shard_map(
        shards,
        mesh=mesh,
        in_specs=(
            P(None, "ep", None),
            P(None, "ep", None),
            P("section", None),
            P("section", None, None),
            P("section", None, "ep"),
            P("section", None, "ep"),
            P("section", "ep", None),
            P("section", None, "ep", None),
            P("section", None, "ep", None),
        ),
        out_specs=(P("section", None, "ep", None), P("section", None, "ep", None)),
        check_vma=False,
    )
```

```python
import functools

import jax
import jax.numpy as jnp
from jax import lax
from jax.experimental import pallas as pl
from jax.experimental.pallas import tpu as pltpu
from jax.sharding import PartitionSpec as P

route_scale = 2.5
epsilon = 1e-06
EXPERT_VMEM = 50
F32 = jnp.float32
BF16 = jnp.bfloat16


def flipped(value, axis, mask):
    count = lax.axis_size(axis)
    return lax.ppermute(value, axis, [(i, i ^ mask) for i in range(count)])


def tied(*values):
    return lax.optimization_barrier(values)


def after(first, *values):
    return lax.optimization_barrier((first, *values))[1:]


def tiles_of(width, wanted=512):
    step = wanted if width % wanted == 0 else width
    return [pl.ds(low, step) for low in range(0, width, step)]


def slot_columns(picks, where, near, geometry):
    tok_count, capacity, room, chips = geometry
    tokens = picks.shape[0]
    base, chip = where[0], where[1] if near else 0
    down = lax.broadcasted_iota(jnp.int32, (tokens, tokens), 0)
    across = lax.broadcasted_iota(jnp.int32, (tokens, tokens), 1)
    earlier = (down // tok_count == across // tok_count) & (across < down)
    chosen = [picks[:, k : k + 1].astype(F32) for k in range(picks.shape[1])]
    rows = [as_row(c, down == across) for c in chosen]
    turn = lax.broadcasted_iota(jnp.int32, (tokens, 1), 0) // tok_count
    columns = []
    for k, own in enumerate(chosen):
        before = sum(jnp.where(earlier & (own == row), 1.0, 0.0) for row in rows)
        place = jnp.sum(before, axis=1, keepdims=True).astype(jnp.int32)
        local = picks[:, k : k + 1] - base
        column = (local ^ chip) * room + turn * capacity + place
        columns.append(jnp.where((local >= 0) & (local < chips), column, -1))
    return columns


def as_row(column, diagonal):
    return jnp.sum(jnp.where(diagonal, column, 0.0), axis=0, keepdims=True)


def start_kernel(near, geometry, where, current, picks, gain, normed, *packed):
    tokens, features = normed.shape
    wide = current[...].astype(F32)
    scale = lax.rsqrt(jnp.mean(wide * wide, axis=-1, keepdims=True) + epsilon)
    normed[...] = (wide * scale * gain[...]).astype(BF16)
    room, chips = geometry[2:]
    down = lax.broadcasted_iota(jnp.int32, (tokens, tokens), 0)
    across = lax.broadcasted_iota(jnp.int32, (tokens, tokens), 1)
    slots = lax.broadcasted_iota(jnp.int32, (chips * room, tokens), 0).astype(F32)
    sender = jnp.zeros(slots.shape, F32)
    for column in slot_columns(picks[...], where, near, geometry):
        sender += jnp.where(slots == as_row(column.astype(F32), down == across), 1.0, 0.0)
    sender = sender.astype(BF16)
    for part in tiles_of(features):
        rows = jnp.dot(sender, normed[:, part], preferred_element_type=F32)
        put_blocks(packed, part, rows.astype(BF16))


def put_blocks(blocks, part, rows):
    room = rows.shape[0] // len(blocks)
    for k, block in enumerate(blocks):
        block[:, part] = rows[k * room : (k + 1) * room]


def get_blocks(blocks, part):
    return jnp.concatenate([block[:, part] for block in blocks], axis=0)


def gate_kernel(turned, geometry, where, near, near_picks, far_picks, scorer, *refs):
    room, chips = geometry[2:]
    *far, mixing = refs
    for place, (parts, picks_ref) in enumerate((((near,), near_picks), (far, far_picks))):
        picks = picks_ref[...]
        tokens, top_count = picks.shape
        raw = [
            lax.dot_general(
                normed[...], scorer[...], (((1,), (1,)), ((), ())), preferred_element_type=F32
            )
            for normed in parts
        ]
        raw = jnp.concatenate(raw, axis=0)
        scores = jax.nn.sigmoid(raw)
        ids = lax.broadcasted_iota(jnp.int32, scores.shape, 1)
        chosen = [
            jnp.sum(jnp.where(ids == picks[:, k : k + 1], scores, 0.0), axis=1, keepdims=True)
            for k in range(top_count)
        ]
        total = sum(chosen)
        slots = lax.broadcasted_iota(jnp.int32, (tokens, chips * room), 1)
        mixed = jnp.zeros(slots.shape, F32)
        for score, column in zip(chosen, slot_columns(picks, where, turned or place == 0, geometry)):
            mixed += jnp.where(slots == column, route_scale * score / total, 0.0)
        high = mixed.astype(BF16)
        mixing[place, 0] = high
        mixing[place, 1] = (mixed - high.astype(F32)).astype(BF16)


def mixed_rows(mixing, place, returned, part):
    rows = get_blocks(returned, part)
    return jnp.dot(mixing[place, 0], rows, preferred_element_type=F32) + jnp.dot(
        mixing[place, 1], rows, preferred_element_type=F32
    )


def far_mix_kernel(mixing, *refs):
    *returned, out = refs
    for part in tiles_of(out.shape[1]):
        out[:, part] = mixed_rows(mixing, 1, returned, part).astype(BF16)


def finish_kernel(mixing, current, beyond, *refs):
    *returned, out = refs
    for part in tiles_of(out.shape[1]):
        near = mixed_rows(mixing, 0, returned, part)
        total = current[:, part].astype(F32) + (near + beyond[:, part].astype(F32))
        out[:, part] = total.astype(BF16)


def last_kernel(section, mixing, current, beyond, first, *refs):
    *returned, rising, falling = refs
    for part in tiles_of(first.shape[1]):
        near = mixed_rows(mixing, 0, returned, part)
        last = current[:, part].astype(F32) + (near + beyond[:, part].astype(F32))
        earlier = first[:, part].astype(F32)
        rising[:, part] = jnp.where(section[0] == 0, earlier, last).astype(BF16)
        falling[:, part] = jnp.where(section[0] == 0, last, earlier).astype(BF16)


def joined_rows(arrived, chips):
    if not chips:
        return get_blocks(arrived, slice(None))
    share = arrived[0].shape[0] // chips
    return jnp.concatenate(
        [piece[k * share : (k + 1) * share] for k in range(chips) for piece in arrived], axis=0
    )


def expert_kernel(sources, chips, *refs):
    arrived, weights, refs = refs[:sources], refs[sources : sources + 6], refs[sources + 6 :]
    *outs, gate_buf, up_buf, down_buf, hidden, sems = refs
    features, units = gate_buf.shape[1:]
    copies = []
    for side in range(2):
        gate_w, up_w, _ = weights[3 * side : 3 * side + 3]
        for part in tiles_of(units, 256):
            copies.append((gate_w.at[:, part], gate_buf.at[side, :, part]))
            copies.append((up_w.at[:, part], up_buf.at[side, :, part]))
    for part in tiles_of(features):
        for side in range(2):
            copies.append((weights[3 * side + 2].at[:, part], down_buf.at[side, :, part]))
    copies = [pltpu.make_async_copy(a, b, sems.at[n]) for n, (a, b) in enumerate(copies)]
    for copy in copies:
        copy.start()
    pending = iter(copies)

    def ready():
        next(pending).wait()
        next(pending).wait()

    held = [buf.at[side] for side in range(2) for buf in (gate_buf, up_buf, down_buf)]
    serve(joined_rows(arrived, chips), held, hidden, outs, ready)


def serve(rows, weights, hidden, outs, ready):
    for side in range(2):
        gate_w, up_w, _ = weights[3 * side : 3 * side + 3]
        for part in tiles_of(hidden.shape[2], 256):
            ready()
            gate_act = jnp.dot(rows, gate_w[:, part], preferred_element_type=F32)
            upward = jnp.dot(rows, up_w[:, part], preferred_element_type=F32)
            hidden[side, :, part] = (jax.nn.silu(gate_act) * upward).astype(BF16)
    for part in tiles_of(outs[0].shape[1]):
        ready()
        total = jnp.dot(hidden[0], weights[2][:, part], preferred_element_type=F32) + jnp.dot(
            hidden[1], weights[5][:, part], preferred_element_type=F32
        )
        put_blocks(outs, part, total.astype(BF16))


VMEM = pl.BlockSpec(memory_space=pltpu.VMEM)
SMEM = pl.BlockSpec(memory_space=pltpu.SMEM)
HBM = pl.BlockSpec(memory_space=pl.ANY)


def shards(
    entering_rising,
    entering_falling,
    norm_gain,
    router,
    w_gate,
    w_up,
    w_down,
    routes_rising,
    routes_falling,
):
    n_section = lax.axis_size("section")
    n_ep = lax.axis_size("ep")
    section_index = lax.axis_index("section")
    ep_index = lax.axis_index("ep")
    micro_count, tok_count, features = entering_rising.shape
    experts = router.shape[2]
    units = w_gate.shape[2]
    top_count = routes_rising.shape[3]
    sharers = n_ep // experts
    capacity = 2 * max(1, tok_count * top_count // experts)
    half = n_ep // 2
    chips = half // sharers
    where = jnp.stack([ep_index // half * chips, ep_index % half // sharers]).astype(jnp.int32)
    scorer = router[0].T
    ticks = jnp.arange(n_section, dtype=jnp.int32)[:, None, None, None]
    picks = jnp.where(section_index == ticks, routes_rising, routes_falling)
    own = (w_gate[0], w_up[0], w_down[0])
    far_picks = flipped(picks, "ep", half)

    tokens = micro_count * tok_count
    room = micro_count * capacity
    geometry = (tok_count, capacity, room, chips)
    block = jax.ShapeDtypeStruct((room, features), BF16)
    packed = jax.ShapeDtypeStruct((chips * room, features), BF16)
    state = jax.ShapeDtypeStruct((tokens, features), BF16)

    def call(kernel, out_shape, in_specs, flops, moved, scratch=(), vmem=24):
        return pl.pallas_call(
            kernel,
            out_shape=out_shape,
            in_specs=in_specs,
            out_specs=jax.tree.map(lambda _: VMEM, out_shape),
            scratch_shapes=scratch,
            compiler_params=pltpu.CompilerParams(vmem_limit_bytes=vmem << 20),
            cost_estimate=pl.CostEstimate(flops=flops, bytes_accessed=moved, transcendentals=0),
        )

    row_bytes = 2 * tokens * features
    pack_flops = 2 * chips * room * tokens * features
    start = call(
        functools.partial(start_kernel, True, geometry),
        [state] + [block] * chips,
        [SMEM, VMEM, VMEM, VMEM],
        pack_flops,
        4 * row_bytes,
    )

    def far_start(cut):
        piece = jax.ShapeDtypeStruct((tokens // cut, features), BF16)
        some = jax.ShapeDtypeStruct((room // cut, features), BF16)
        return call(
            functools.partial(start_kernel, True, (tok_count, capacity, room // cut, chips)),
            [piece] + [some] * chips,
            [SMEM, VMEM, VMEM, VMEM],
            pack_flops // cut,
            4 * row_bytes // cut,
        )

    def gates(cut):
        return call(
            functools.partial(gate_kernel, True, geometry),
            jax.ShapeDtypeStruct((2, 2, tokens, chips * room), BF16),
            [SMEM] + [VMEM] * (4 + cut),
            4 * tokens * features * 128,
            2 * row_bytes,
        )

    def expert(sources, joined, shapes):
        return call(
            functools.partial(expert_kernel, sources, joined),
            shapes,
            [VMEM] * sources + [HBM] * 6,
            12 * chips * room * features * units,
            12 * features * units,
            [
                pltpu.VMEM((2, features, units), BF16),
                pltpu.VMEM((2, features, units), BF16),
                pltpu.VMEM((2, units, features), BF16),
                pltpu.VMEM((2, chips * room, units), BF16),
                pltpu.SemaphoreType.DMA(
                    (4 * len(tiles_of(units, 256)) + 2 * len(tiles_of(features)),)
                ),
            ],
            EXPERT_VMEM,
        )

    def far_mix(mixing, *returned):
        specs = [VMEM] * (1 + len(returned))
        return call(far_mix_kernel, state, specs, 2 * pack_flops, 3 * row_bytes)(mixing, *returned)

    finish_last = call(
        last_kernel, [state] * 2, [SMEM] + [VMEM] * (4 + chips), 2 * pack_flops, 7 * row_bytes
    )
    finish = call(
        finish_kernel, state, [VMEM] * (3 + chips), 2 * pack_flops, 5 * row_bytes)
    circles = [
        [low + core + sharers * k for k in range(chips)] for low in (0, half) for core in range(sharers)
    ]

    def spread(rows):
        return lax.all_to_all(
            rows, "ep", split_axis=0, concat_axis=0, tiled=True, axis_index_groups=circles
        )

    def pass_on(blocks):
        return [blocks[0]] + [flipped(blocks[k], "ep", sharers * k) for k in range(1, chips)]

    def layer(current, far_current, picks, far_picks, weights):
        normed, *near_rows = start(where, current, picks, norm_gain)
        far_current = list(far_current)
        pieces = len(far_current)
        far_current[-1], *near_rows = tied(far_current[-1], *near_rows)
        far_in, far_normed = [], []
        for states, chosen in zip(far_current, jnp.split(far_picks, pieces)):
            part, *rows = far_start(pieces)(where, states, chosen, norm_gain)
            far_normed.append(part)
            far_in.append(pass_on(rows))
        mixing = gates(pieces)(where, normed, picks, far_picks, scorer, *far_normed)
        far_in = [piece[k] for k in range(chips) for piece in far_in]
        far_in[-1], mixing, *near_rows = tied(far_in[-1], mixing, *near_rows)
        far_out = list(expert(len(far_in), 0, [block] * chips)(*far_in, *weights))
        far_out[-1], *near_in = tied(far_out[-1], *pass_on(near_rows))
        near_out = expert(chips, 0, [block] * chips)(*near_in, *weights)
        far_part, *near_out = tied(far_mix(mixing, *pass_on(far_out)), *near_out)
        beyond = flipped(far_part, "ep", half)
        return mixing, current, beyond, pass_on(near_out)

    tables = [a.reshape(n_section, tokens, top_count) for a in (picks, far_picks)]

    def advance(tick, current, far_current, weights):
        here = [lax.dynamic_index_in_dim(a, tick, 0, keepdims=False) for a in tables]
        return layer(current, far_current, *here, weights)

    def whole_weights(*own):
        return (*own, *[flipped(w, "ep", 1) for w in own])

    entered = jnp.where(section_index == 0, entering_rising, entering_falling)
    entered = entered.reshape(tokens, features)
    pieces = 2 if room % 32 == 0 and n_section == 2 else 1
    far = [flipped(e, "ep", half) for e in jnp.split(entered, pieces)]
    weights = whole_weights(*own)
    if n_section == 2:
        mixing, current, beyond, returned = advance(0, entered, far, weights)
        first = finish(mixing, current, beyond, *returned)
        across = [(i, (i + n_ep) % (2 * n_ep) ^ half) for i in range(2 * n_ep)]
        far = [lax.ppermute(first, ("section", "ep"), across)]
        mixing, current, beyond, returned = advance(1, flipped(first, "section", 1), far, weights)
        here = section_index.astype(jnp.int32)[None]
        kept_rising, kept_falling = finish_last(here, mixing, current, beyond, first, *returned)
    else:

        def body(tick, carry):
            current, far, kept_rising, kept_falling = carry
            mixing, current, beyond, returned = advance(tick, current, far, weights)
            done = finish(mixing, current, beyond, *returned)
            kept_rising = jnp.where(section_index == tick, done, kept_rising)
            kept_falling = jnp.where(section_index == n_section - 1 - tick, done, kept_falling)
            up = lax.ppermute(done, "section", [(i, i + 1) for i in range(n_section - 1)])
            down = lax.ppermute(done, "section", [(i + 1, i) for i in range(n_section - 1)])
            current = jnp.where(section_index == tick + 1, up, down)
            far = [flipped(current, "ep", half)]
            return current, far, kept_rising, kept_falling

        empty = jnp.zeros((tokens, features), BF16)
        _, _, kept_rising, kept_falling = lax.fori_loop(
            0, n_section, body, (entered, far, empty, empty)
        )
    out = (1, micro_count, tok_count, features)
    return (
        kept_rising.reshape(out),
        kept_falling.reshape(out),
    )


def solution(mesh):
    return jax.shard_map(
        shards,
        mesh=mesh,
        in_specs=(
            P(None, "ep", None),
            P(None, "ep", None),
            P("section", None),
            P("section", None, None),
            P("section", None, "ep"),
            P("section", None, "ep"),
            P("section", "ep", None),
            P("section", None, "ep", None),
            P("section", None, "ep", None),
        ),
        out_specs=(P("section", None, "ep", None), P("section", None, "ep", None)),
        check_vma=False,
    )
```
